256 devices in a mesh: segment: 4 (over x), tok: 64 (over z, y, core).
Axes of the slice: x: 4, y: 4, z: 8, core: 2. Of those that a mesh axis runs over, the one named last changes fastest.
Arguments:
- point_feats: bfloat16 [4, 256, 64, 8, 8], P(None, ('segment', 'tok')), may hold values from -6 to 6
- point_voxel: int32 [4, 256, 64, 8], P(None, ('segment', 'tok')), may hold values from 0 to 4095
- send_counts: int32 [4, 256, 64], P(None, ('segment', 'tok')), may hold values from 0 to 8, as said below
- tok_weight: bfloat16 [2048, 512], P('segment'), may hold values from -0.125 to 0.125
- tok_gain: float32 [512], replicated, may hold values from 0.1 to 1.9
- dec_weight: bfloat16 [512, 2048], P(None, 'segment'), may hold values from -0.25 to 0.25
- dec_gain: float32 [512], replicated, may hold values from 0.1 to 1.9
- attn_gain: float32 [4, 512], P('segment'), may hold values from 0.1 to 1.9
- mlp_gain: float32 [4, 512], P('segment'), may hold values from 0.1 to 1.9
- query_gain: float32 [4, 64], P('segment'), may hold values from 0.1 to 1.9
- key_gain: float32 [4, 64], P('segment'), may hold values from 0.1 to 1.9
- qkv_weight: bfloat16 [4, 512, 1536], P('segment'), may hold values from -0.25 to 0.25
- out_weight: bfloat16 [4, 512, 512], P('segment'), may hold values from -0.25 to 0.25
- in_weight: bfloat16 [4, 512, 2048], P('segment'), may hold values from -0.25 to 0.25
- down_weight: bfloat16 [4, 2048, 512], P('segment'), may hold values from -0.125 to 0.125
Outputs:
- predictions: bfloat16 [3, 4, 1024, 2048], P(None, None, 'tok', 'segment')
The draws below stay inside these ranges and needn't reach their ends.
Inputs may be any that keep to these rules, and one draw needn't show every extreme that they name: `send_counts`: slots past the count hold unused values. In every draw and scene some tile receives 8 points from every sender. `point_voxel`: local token of the destination tile times 256 plus the voxel within that token's patch.
All inputs are finite; a program needn't handle non-finite values.
Results may differ from the reference program's by a relative error of at most 0.03.
Values may be sent and summed in bfloat16 or wider, within the bound.
No kernel may reach another device: no remote copies, remote signals or barrier semaphores. Data moves between devices by JAX's collectives and lax.ppermute only.
A program may use at most 64 MiB of HBM per device.

```python
import math
import jax
import jax.numpy as jnp
from jax import lax

D = 512
FF = 2048
HEADS = 8
HD = 64
PF = 8
VOX = 256
VQ = 64
VOXCH = 2048
LAYERS = 4
ROLL = 3
CAP = 8
TOK_DEV = 16
SCENES = 4
TILES = 64
SENDERS = 256
TOKENS = 1024
N_SEGMENT = 4


def draw_send_counts(key, part):
    key = jax.random.fold_in(key, 7)
    base_key, boost_key, dense_key = jax.random.split(key, 3)
    base_load = jax.random.randint(base_key, (SCENES, SENDERS, TILES), 0, CAP // 2 + 1)
    boost_load = jax.random.randint(boost_key, (SCENES, 1, TILES), 0, CAP + 1)
    dense_tile = jax.random.randint(dense_key, (SCENES, 1, 1), 0, TILES)
    tile_ids = jnp.arange(TILES)[None, None, :]
    slot_count = jnp.minimum(base_load + boost_load, CAP)
    return jnp.where(tile_ids == dense_tile, CAP, slot_count).astype(jnp.int32)


def with_ends(entries, key, least, high):
    index_at = [jax.random.randint(jax.random.fold_in(key, axis), (), 0, length) for axis, length in enumerate(entries.shape)]
    longest = entries.shape.index(max(entries.shape))
    neighbour = index_at[:longest] + [(index_at[longest] + 1) % entries.shape[longest]] + index_at[longest + 1:]
    return entries.at[tuple(index_at)].set(least).at[tuple(neighbour)].set(high)


def level_of(rng, dims, cuts, low, high):
    factor_of, own = 1.0, jax.random.fold_in(rng, 6)
    for position, blocks in cuts:
        heights = jnp.exp(jax.random.uniform(jax.random.fold_in(own, position), (blocks,), jnp.float32, low / len(cuts), high / len(cuts)))
        factor_of = factor_of * jnp.repeat(heights, dims[position] // blocks).reshape([-1 if axis == position else 1 for axis in range(len(dims))])
    return factor_of


def noise(own_key, shape, spread, limit, pieces=(), held_as=jnp.bfloat16):
    result = spread * jax.random.normal(own_key, shape, jnp.float32)
    if pieces:
        result = result * level_of(own_key, shape, pieces, -0.22, 0.18)
    return jnp.clip(result, -limit, limit).astype(held_as)


def setup_inputs(seed: int = 0) -> dict:
    splits = jax.random.split(jax.random.key(seed), 16)
    return {
        "point_feats": noise(splits[0], (SCENES, SENDERS, TILES, CAP, PF), 1.0, 6.0, ((1, 256),)),
        "point_voxel": with_ends(jax.random.randint(splits[1], (SCENES, SENDERS, TILES, CAP), 0, TOK_DEV * VOX), jax.random.fold_in(splits[1], 1), 0, (TOK_DEV * VOX) - 1).astype(jnp.int32),
        "send_counts": draw_send_counts(jax.random.fold_in(splits[15], 71), 0),
        "tok_weight": noise(splits[3], (VOXCH, D), VOXCH ** -0.5, 0.125, ((0, 4),)),
        "tok_gain": jnp.clip(1.0 + 0.18 * jax.random.normal(splits[4], (D,), jnp.float32), 0.1, 1.9),
        "dec_weight": noise(splits[5], (D, VOXCH), D ** -0.5, 0.25, ((1, 4),)),
        "dec_gain": jnp.clip(1.0 + 0.18 * jax.random.normal(splits[6], (D,), jnp.float32), 0.1, 1.9),
        "attn_gain": jnp.clip(1.0 + 0.18 * jax.random.normal(splits[7], (LAYERS, D), jnp.float32), 0.1, 1.9),
        "mlp_gain": jnp.clip(1.0 + 0.18 * jax.random.normal(splits[8], (LAYERS, D), jnp.float32), 0.1, 1.9),
        "query_gain": jnp.clip(1.0 + 0.18 * jax.random.normal(splits[9], (LAYERS, HD), jnp.float32), 0.1, 1.9),
        "key_gain": jnp.clip(1.0 + 0.18 * jax.random.normal(splits[10], (LAYERS, HD), jnp.float32), 0.1, 1.9),
        "qkv_weight": noise(splits[11], (LAYERS, D, 3 * D), D ** -0.5, 0.25, ((0, 4),)),
        "out_weight": noise(splits[12], (LAYERS, D, D), D ** -0.5, 0.25, ((0, 4),)),
        "in_weight": noise(splits[13], (LAYERS, D, FF), D ** -0.5, 0.25, ((0, 4),)),
        "down_weight": noise(splits[14], (LAYERS, FF, D), FF ** -0.5, 0.125, ((0, 4),)),
    }


EPSILON = 1e-06

def rms_scale(tensor, factor):
    return tensor * lax.rsqrt(lax.optimization_barrier(jnp.mean(tensor * tensor, axis=-1, keepdims=True)) + EPSILON) * factor

def head_scale(tensor, factor):
    shaped = tensor.reshape(tensor.shape[:-1] + (HEADS, HD))
    return rms_scale(shaped, factor)

def held(tensor):
    return lax.optimization_barrier(tensor.astype(jnp.bfloat16))

def dot_rows(tensor, weight):
    flat = jnp.dot(tensor.reshape(-1, tensor.shape[-1]), weight, preferred_element_type=jnp.float32)
    return flat.reshape(tensor.shape[:-1] + (weight.shape[-1],))

def tokenize(voxels, tok_weight, tok_gain):
    return rms_scale(dot_rows(voxels, tok_weight), tok_gain).astype(jnp.bfloat16)

def attention(queries, key_rows, value_rows):
    padded_keys = jnp.pad(key_rows.astype(jnp.float32), ((0, 0), (TOK_DEV, TOK_DEV), (0, 0), (0, 0)))
    padded_values = jnp.pad(value_rows.astype(jnp.float32), ((0, 0), (TOK_DEV, TOK_DEV), (0, 0), (0, 0)))
    query_all = queries.astype(jnp.float32)

    def one_block(block_no):
        first_row = block_no * TOK_DEV
        query_block = lax.dynamic_slice_in_dim(query_all, first_row, TOK_DEV, 1)
        key_block = lax.dynamic_slice_in_dim(padded_keys, first_row, 3 * TOK_DEV, 1)
        value_block = lax.dynamic_slice_in_dim(padded_values, first_row, 3 * TOK_DEV, 1)
        query_pos = first_row + jnp.arange(TOK_DEV, dtype=jnp.int32)
        key_pos = first_row - TOK_DEV + jnp.arange(3 * TOK_DEV, dtype=jnp.int32)
        near = jnp.abs(query_pos[:, None] - key_pos[None, :]) <= TOK_DEV
        inside = (key_pos >= 0) & (key_pos < TOKENS)
        gate = (near & inside[None, :]).astype(jnp.float32)
        scores = jnp.einsum('sqhd,skhd->shqk', query_block, key_block, precision=lax.Precision.HIGHEST) / math.sqrt(HD)
        weights = jnp.exp(scores) * gate
        attn_probs = held(weights / lax.optimization_barrier(jnp.sum(weights, axis=-1, keepdims=True))).astype(jnp.float32)
        blended = jnp.einsum('shqk,skhd->sqhd', attn_probs, value_block, precision=lax.Precision.HIGHEST)
        return blended.astype(jnp.bfloat16)
    blocks = lax.map(one_block, jnp.arange(TOKENS // TOK_DEV, dtype=jnp.int32))
    return blocks.transpose(1, 0, 2, 3, 4).reshape(SCENES, TOKENS, D)

def reference(point_feats, point_voxel, send_counts, tok_weight, tok_gain, dec_weight, dec_gain, attn_gain, mlp_gain, query_gain, key_gain, qkv_weight, out_weight, in_weight, down_weight):
    live_slot = jnp.arange(CAP, dtype=jnp.int32)[None, None, None, :] < send_counts[..., None]
    tile_ids = jnp.arange(TILES, dtype=jnp.int32)[None, None, :, None]
    token_ids = tile_ids * TOK_DEV + point_voxel // VOX
    within = point_voxel % VOX
    target = (token_ids * VOX + within).reshape(SCENES, -1)
    features = jnp.where(live_slot[..., None], point_feats.astype(jnp.float32), jnp.zeros((), jnp.float32))
    features = features.reshape(SCENES, -1, PF)

    def one_scene(scene_pair):
        scene_target, scene_features = scene_pair
        return jnp.zeros((TOKENS * VOX, PF), jnp.float32).at[scene_target].add(scene_features)
    voxel_grid = lax.map(one_scene, (target, features))
    voxel_grid = voxel_grid.reshape(SCENES, TOKENS, N_SEGMENT, VQ, PF).transpose(0, 1, 2, 4, 3).reshape(SCENES, TOKENS, VOXCH)
    frame_input = tokenize(voxel_grid.astype(jnp.bfloat16), tok_weight, tok_gain)
    predictions = []
    for frame_index in range(ROLL):
        stream = frame_input.astype(jnp.float32)
        for layer_no in range(LAYERS):
            normed = rms_scale(stream, attn_gain[layer_no]).astype(jnp.bfloat16)
            projected = dot_rows(normed, qkv_weight[layer_no])
            queries = held(head_scale(projected[..., :D], query_gain[layer_no]))
            key_rows = held(head_scale(projected[..., D:2 * D], key_gain[layer_no]))
            value_rows = held(projected[..., 2 * D:].reshape(SCENES, TOKENS, HEADS, HD))
            blended = attention(queries, key_rows, value_rows)
            attended = stream + dot_rows(blended, out_weight[layer_no])
            normed_ff = rms_scale(attended, mlp_gain[layer_no]).astype(jnp.bfloat16)
            hidden = jax.nn.gelu(dot_rows(normed_ff, in_weight[layer_no])).astype(jnp.bfloat16)
            stream = attended + dot_rows(hidden, down_weight[layer_no])
        normed_dec = rms_scale(stream, dec_gain).astype(jnp.bfloat16)
        predicted = jnp.tanh(dot_rows(normed_dec, dec_weight)).astype(jnp.bfloat16)
        predictions.append(predicted)
        frame_input = tokenize(predicted, tok_weight, tok_gain)
    return jnp.stack(predictions)
```

```python
import functools

import jax
import jax.numpy as jnp
from jax import lax
from jax.experimental import pallas as pl
from jax.experimental.pallas import tpu as pltpu
from jax.sharding import PartitionSpec as P

LAYERS = 4
ROLL = 3
TOK_DEV = 16
TILES = 64
TOKENS = TILES * TOK_DEV
WIDTH = 512
HEADS = 8
HEAD_DIM = 64
SECTIONS = 4
SLOTS = 8
CHANNELS = 8
HALO = LAYERS
EPSILON = 1e-06

F32 = jnp.float32
BF16 = jnp.bfloat16

QKV, OUT, IN, DOWN, DEC, TOK = range(6)
WEIGHT_ROWS = (512, 512, 512, 2048, 512, 512)
WEIGHT_COLS = (1536, 512, 2048, 512, 512, 512)


def rms_scale(tensor, factor):
    return tensor * lax.rsqrt(jnp.mean(tensor * tensor, axis=-1, keepdims=True) + EPSILON) * factor


def dot(left, right):
    return jnp.dot(left, right, preferred_element_type=F32)


def dot_t(left, right):
    return lax.dot_general(left, right, (((1,), (1,)), ((), ())), preferred_element_type=F32)


def low_lanes(shape):
    return lax.broadcasted_iota(jnp.int32, shape, 1) % 128 < HEAD_DIM


def head_scale(tensor, factor, pool):
    parts = []
    for start in range(0, WIDTH, 256):
        part = tensor[:, start : start + 256]
        mean = dot((part * part).astype(BF16), pool)
        parts.append(part * lax.rsqrt(mean + EPSILON))
    return (jnp.concatenate(parts, axis=1) * factor).astype(BF16)


def attention(queries, key_rows, value_rows, near):
    rows = queries.shape[0]
    low = low_lanes((rows, 128))
    zero = jnp.zeros((rows, 128), BF16)
    outs = []
    for pair in range(HEADS // 2):
        cols = slice(128 * pair, 128 * pair + 128)
        both = queries[:, cols]
        stacked = jnp.concatenate([jnp.where(low, both, zero), jnp.where(low, zero, both)], axis=0)
        weights = jnp.where(near, jnp.exp(dot_t(stacked, key_rows[:, cols])), 0.0)
        total = jnp.maximum(jnp.sum(weights, axis=-1, keepdims=True), 1e-30)
        probs = (weights / total).astype(BF16)
        mixed = dot(probs, value_rows[:, cols])
        outs.append(jnp.where(low, mixed[:rows], mixed[rows:]))
    return jnp.concatenate(outs, axis=1).astype(BF16)


def near_mask(tile, halo, rows, keys):
    query = lax.broadcasted_iota(jnp.int32, (2 * rows, keys), 0) % rows + TOK_DEV
    key = lax.broadcasted_iota(jnp.int32, (2 * rows, keys), 1)
    position = (tile - halo) * TOK_DEV + key
    return (jnp.abs(query - key) <= TOK_DEV) & (position >= 0) & (position < TOKENS)


def frame_kernel(with_next, *refs):
    (tile_ref, x_ref, gains_ref, heads_ref, dec_gain_ref, tok_gain_ref), refs = refs[:6], refs[6:]
    halves, refs = refs[:12], refs[12:]
    if with_next:
        (pred_ref, next_ref), refs = refs[:2], refs[2:]
    else:
        (pred_ref,), refs = refs[:1], refs[1:]
    slots, sems = refs[:6], refs[6]
    tile = tile_ref[0]
    core = tile % 2

    def copies(kind, index):
        half = WEIGHT_COLS[kind] // 2
        rows = WEIGHT_ROWS[kind]
        made = []
        for side in range(2):
            column = jnp.where(side == 0, core, 1 - core) * half
            if kind in (DEC, TOK):
                column = column + (index * 512 if kind == DEC else 0)
                place = slots[kind].at[
                    pl.ds(index * rows if kind == TOK else 0, rows),
                    pl.ds(pl.multiple_of(column, 128), half),
                ]
            else:
                place = slots[kind].at[index, :, pl.ds(pl.multiple_of(column, 128), half)]
            made.append(
                pltpu.make_async_copy(
                    halves[2 * kind + side].at[pl.ds(index * rows, rows), :],
                    place,
                    sems.at[kind, index, side],
                )
            )
        return made

    def begin(kind, index):
        for copy in copies(kind, index):
            copy.start()

    def ready(kind, index):
        for copy in copies(kind, index):
            copy.wait()

    for layer in range(LAYERS):
        for kind in (QKV, OUT, IN, DOWN):
            begin(kind, layer)
    for kind in (DEC, TOK) if with_next else (DEC,):
        for section in range(SECTIONS):
            begin(kind, section)

    row = lax.broadcasted_iota(jnp.int32, (256, 256), 0) // HEAD_DIM
    col = lax.broadcasted_iota(jnp.int32, (256, 256), 1) // HEAD_DIM
    pool = jnp.where(row == col, 1.0 / HEAD_DIM, 0.0).astype(BF16)

    stream = x_ref[...].astype(F32)
    for layer in range(LAYERS):
        halo = LAYERS - layer
        keys = (2 * halo + 1) * TOK_DEV
        rows = keys - 2 * TOK_DEV
        own = slice(TOK_DEV, TOK_DEV + rows)
        normed = rms_scale(stream, gains_ref[layer : layer + 1, :]).astype(BF16)
        ready(QKV, layer)
        projected = dot(normed, slots[QKV][layer])
        queries = head_scale(projected[own, :WIDTH], heads_ref[layer : layer + 1, :], pool)
        key_rows = head_scale(
            projected[:, WIDTH : 2 * WIDTH], heads_ref[LAYERS + layer : LAYERS + layer + 1, :], pool
        )
        value_rows = projected[:, 2 * WIDTH :].astype(BF16)
        blended = attention(queries, key_rows, value_rows, near_mask(tile, halo, rows, keys))
        ready(OUT, layer)
        attended = stream[own] + dot(blended, slots[OUT][layer])
        normed_ff = rms_scale(attended, gains_ref[LAYERS + layer : LAYERS + layer + 1, :])
        ready(IN, layer)
        hidden = jax.nn.gelu(dot(normed_ff.astype(BF16), slots[IN][layer])).astype(BF16)
        ready(DOWN, layer)
        stream = attended + dot(hidden, slots[DOWN][layer])

    normed_dec = rms_scale(stream, dec_gain_ref[...]).astype(BF16)
    for section in range(SECTIONS):
        ready(DEC, section)
    predicted = jnp.tanh(dot(normed_dec, slots[DEC][...])).astype(BF16)
    for section in range(SECTIONS):
        pred_ref[section] = predicted[:, section * 512 : section * 512 + 512]
    if with_next:
        for section in range(SECTIONS):
            ready(TOK, section)
        upcoming = rms_scale(dot(predicted, slots[TOK][...]), tok_gain_ref[...])
        next_ref[...] = upcoming.astype(BF16)


def frame(tile, rows, gains, head_gains, dec_gain, tok_gain, halves, with_next):
    vmem = pl.BlockSpec(memory_space=pltpu.VMEM)
    out_shape = [jax.ShapeDtypeStruct((SECTIONS, TOK_DEV, 512), BF16)]
    if with_next:
        out_shape.append(jax.ShapeDtypeStruct((TOK_DEV, WIDTH), BF16))
    return pl.pallas_call(
        functools.partial(frame_kernel, with_next),
        out_shape=out_shape,
        in_specs=[pl.BlockSpec(memory_space=pltpu.SMEM)]
        + [vmem] * 5
        + [pl.BlockSpec(memory_space=pl.ANY)] * 12,
        out_specs=[vmem] * len(out_shape),
        scratch_shapes=[
            pltpu.VMEM((LAYERS, 512, 1536), BF16),
            pltpu.VMEM((LAYERS, 512, 512), BF16),
            pltpu.VMEM((LAYERS, 512, 2048), BF16),
            pltpu.VMEM((LAYERS, 2048, 512), BF16),
            pltpu.VMEM((512, 2048), BF16),
            pltpu.VMEM((2048, 512), BF16),
            pltpu.SemaphoreType.DMA((6, 4, 2)),
        ],
        compiler_params=pltpu.CompilerParams(vmem_limit_bytes=52 * 1024 * 1024),
        name="frame",
    )(tile, rows, gains, head_gains, dec_gain, tok_gain, *halves)


def scatter_kernel(tile_ref, points_ref, tok_gain_ref, mine_ref, other_ref, out_ref, tok_ref, sems):
    core = tile_ref[0] % 2

    def copies():
        return [
            pltpu.make_async_copy(
                half_ref,
                tok_ref.at[:, pl.ds(pl.multiple_of(column * 256, 128), 256)],
                sems.at[side],
            )
            for side, (half_ref, column) in enumerate(((mine_ref, core), (other_ref, 1 - core)))
        ]

    for copy in copies():
        copy.start()
    turned = jnp.transpose(points_ref[...].astype(F32))
    senders = turned.shape[1]
    cell_ids = lax.broadcasted_iota(jnp.int32, (64, senders), 0).astype(F32)
    voxel_ids = (lax.broadcasted_iota(jnp.int32, (128, senders), 0) % 64).astype(F32)
    totals = jnp.zeros((CHANNELS * 64, 128), F32)
    for slot in range(SLOTS):
        cell = turned[64 + slot : 65 + slot, :]
        voxel = turned[72 + slot : 73 + slot, :]
        here = cell_ids == cell
        picked = jnp.where(voxel_ids == voxel, 1.0, 0.0).astype(BF16)
        weighted = jnp.concatenate(
            [
                jnp.where(here, turned[slot * CHANNELS + e : slot * CHANNELS + e + 1, :], 0.0)
                for e in range(CHANNELS)
            ],
            axis=0,
        ).astype(BF16)
        totals = totals + dot_t(weighted, picked)
    low = low_lanes((TOK_DEV, 128))
    columns = []
    for section in range(SECTIONS):
        for e in range(0, CHANNELS, 2):
            first = e * 64 + section * TOK_DEV
            second = first + 64
            columns.append(
                jnp.where(low, totals[first : first + TOK_DEV], totals[second : second + TOK_DEV])
            )
    grid = jnp.concatenate(columns, axis=1).astype(BF16)
    for copy in copies():
        copy.wait()
    out_ref[...] = rms_scale(dot(grid, tok_ref[...]), tok_gain_ref[...]).astype(BF16)


def scatter(tile, points, tok_gain, mine, other):
    vmem = pl.BlockSpec(memory_space=pltpu.VMEM)
    return pl.pallas_call(
        scatter_kernel,
        out_shape=jax.ShapeDtypeStruct((TOK_DEV, WIDTH), BF16),
        in_specs=[pl.BlockSpec(memory_space=pltpu.SMEM), vmem, vmem]
        + [pl.BlockSpec(memory_space=pl.ANY)] * 2,
        out_specs=vmem,
        scratch_shapes=[pltpu.VMEM((2048, 512), BF16), pltpu.SemaphoreType.DMA((2,))],
        compiler_params=pltpu.CompilerParams(vmem_limit_bytes=32 * 1024 * 1024),
        name="scatter",
    )(tile, points, tok_gain, mine, other)


def sibling(block):
    return lax.ppermute(block, "tok", [(i, i ^ 1) for i in range(TILES)])


def gather_half(weight):
    tile = lax.axis_index("tok")
    rows, cols = weight.shape
    piece = lax.dynamic_slice(
        weight, (tile // 2 * (rows // 32), tile % 2 * (cols // 2)), (rows // 32, cols // 2)
    )
    groups = [
        [s * TILES + zy * 2 + core for s in range(SECTIONS) for zy in range(TILES // 2)]
        for core in range(2)
    ]
    return lax.all_gather(piece, ("segment", "tok"), axis_index_groups=groups, tiled=True)


def with_halo(block):
    blocks = []
    for shift in range(-HALO, HALO + 1):
        if shift == 0:
            blocks.append(block)
        else:
            route = [(i + shift, i) for i in range(TILES) if 0 <= i + shift < TILES]
            blocks.append(lax.ppermute(block, "tok", route))
    return jnp.concatenate(blocks, axis=0)


def send_points(point_feats, point_voxel, send_counts):
    feats = point_feats.reshape(SECTIONS * TILES, SLOTS * CHANNELS)
    voxel = point_voxel.reshape(SECTIONS * TILES, SLOTS)
    counts = send_counts.reshape(SECTIONS * TILES, 1)
    live = jnp.arange(SLOTS)[None, :] < counts
    cell = jnp.where(live, voxel // 64 % SECTIONS * TOK_DEV + voxel // 256, -1).astype(BF16)
    inner = (voxel % 64).astype(BF16)
    message = jnp.concatenate(
        [feats, cell, inner, jnp.zeros((SECTIONS * TILES, 48), BF16)], axis=1
    )
    return lax.all_to_all(message, ("segment", "tok"), split_axis=0, concat_axis=0, tiled=True)


def local(
    point_feats,
    point_voxel,
    send_counts,
    tok_weight,
    tok_gain,
    dec_weight,
    dec_gain,
    attn_gain,
    mlp_gain,
    query_gain,
    key_gain,
    qkv_weight,
    out_weight,
    in_weight,
    down_weight,
):
    tile = lax.axis_index("tok").astype(jnp.int32).reshape(1)
    points = send_points(point_feats, point_voxel, send_counts)
    own_gains = jnp.concatenate([attn_gain, mlp_gain, query_gain, key_gain], axis=1)
    all_gains = lax.all_to_all(
        jnp.broadcast_to(own_gains, (SECTIONS, own_gains.shape[1])),
        "segment",
        split_axis=0,
        concat_axis=0,
        tiled=True,
    )
    gains = jnp.concatenate([all_gains[:, :512], all_gains[:, 512:1024]], axis=0)
    head_gains = jnp.concatenate(
        [
            jnp.tile(all_gains[:, 1024:1088], (1, HEADS)) * 0.125,
            jnp.tile(all_gains[:, 1088:], (1, HEADS)),
        ],
        axis=0,
    )
    halves = []
    for weight in (qkv_weight[0], out_weight[0], in_weight[0], down_weight[0], dec_weight, tok_weight):
        mine = gather_half(weight)
        halves += [mine, sibling(mine)]
    tok_gain = tok_gain[None]
    dec_gain = dec_gain[None]
    entering = scatter(tile, points, tok_gain, halves[10], halves[11])
    frames = []
    for frame_index in range(ROLL):
        with_next = frame_index + 1 < ROLL
        made = frame(
            tile,
            with_halo(entering),
            gains,
            head_gains,
            dec_gain,
            tok_gain,
            halves,
            with_next,
        )
        frames.append(
            lax.all_to_all(made[0], "segment", split_axis=0, concat_axis=0, tiled=True)
        )
        if with_next:
            entering = made[1]
    return jnp.stack(frames)


def solution(mesh):
    return jax.shard_map(
        local,
        mesh=mesh,
        in_specs=(
            P(None, ("segment", "tok"), None, None, None),
            P(None, ("segment", "tok"), None, None),
            P(None, ("segment", "tok"), None),
            P("segment", None),
            P(),
            P(None, "segment"),
            P(),
            P("segment", None),
            P("segment", None),
            P("segment", None),
            P("segment", None),
            P("segment", None, None),
            P("segment", None, None),
            P("segment", None, None),
            P("segment", None, None),
        ),
        out_specs=P(None, None, "tok", "segment"),
        check_vma=False,
    )
```

```python
import functools

import jax
import jax.numpy as jnp
from jax import lax
from jax.experimental import pallas as pl
from jax.experimental.pallas import tpu as pltpu
from jax.sharding import PartitionSpec as P

LAYERS = 4
ROLL = 3
TOK_DEV = 16
TILES = 64
TOKENS = TILES * TOK_DEV
WIDTH = 512
HEADS = 8
HEAD_DIM = 64
SECTIONS = 4
SLOTS = 8
CHANNELS = 8
HALO = ROLL * LAYERS
EPSILON = 1e-06

F32 = jnp.float32
BF16 = jnp.bfloat16


def rms_scale(tensor, factor):
    return tensor * lax.rsqrt(jnp.mean(tensor * tensor, axis=-1, keepdims=True) + EPSILON) * factor


def dot(left, right):
    return jnp.dot(left, right, preferred_element_type=F32)


def dot_t(left, right):
    return lax.dot_general(left, right, (((1,), (1,)), ((), ())), preferred_element_type=F32)


def low_lanes(shape):
    return lax.broadcasted_iota(jnp.int32, shape, 1) % 128 < HEAD_DIM


def head_scale(tensor, factor, pool):
    parts = []
    for start in range(0, WIDTH, 256):
        part = tensor[:, start : start + 256]
        mean = dot((part * part).astype(BF16), pool)
        parts.append(part * lax.rsqrt(mean + EPSILON))
    return (jnp.concatenate(parts, axis=1) * factor).astype(BF16)


def attention(queries, key_rows, value_rows, near):
    rows = queries.shape[0]
    low = low_lanes((rows, 128))
    zero = jnp.zeros((rows, 128), BF16)
    outs = []
    for pair in range(HEADS // 2):
        cols = slice(128 * pair, 128 * pair + 128)
        both = queries[:, cols]
        stacked = jnp.concatenate([jnp.where(low, both, zero), jnp.where(low, zero, both)], axis=0)
        weights = jnp.where(near, jnp.exp(dot_t(stacked, key_rows[:, cols])), 0.0)
        total = jnp.maximum(jnp.sum(weights, axis=-1, keepdims=True), 1e-30)
        probs = (weights * (1.0 / total)).astype(BF16)
        mixed = dot(probs, value_rows[:, cols])
        outs.append(jnp.where(low, mixed[:rows], mixed[rows:]))
    return jnp.concatenate(outs, axis=1).astype(BF16)


def near_mask(first_position, rows, keys):
    query = lax.broadcasted_iota(jnp.int32, (2 * rows, keys), 0) % rows + TOK_DEV
    key = lax.broadcasted_iota(jnp.int32, (2 * rows, keys), 1)
    position = first_position + key
    return (jnp.abs(query - key) <= TOK_DEV) & (position >= 0) & (position < TOKENS)


QKV, OUT, IN, DOWN, DEC, TOK = range(6)


def start_weights(section, tile, own, tok_all, a_mine, a_other, c_mine, c_other, e_mine, e_other, slots, sems):
    core = tile % 2
    column = tile // 2 % 4
    qkv, out, up, down, dec, tok = slots

    def start(source, target, kind, layer):
        pltpu.make_async_copy(source, target, sems.at[kind, layer]).start()

    for layer in range(LAYERS):
        behind = lax.rem(section + LAYERS - layer, LAYERS)

        @pl.when(behind == 0)
        def _():
            for kind in (QKV, OUT, IN, DOWN, DEC):
                start(own[kind], slots[kind].at[layer], kind, layer)

        for step in range(1, LAYERS):

            @pl.when(behind == step)
            def _():
                for part, side in ((a_mine, core), (a_other, 1 - core)):
                    start(part[step - 1], qkv.at[layer, pl.ds(pl.multiple_of(side * 256, 256), 256)], QKV, layer)

        @pl.when(behind != 0)
        def _():
            index = jnp.maximum(behind - 1, 0)
            pieces = []
            for shift in range(4):
                origin = lax.rem(column + 4 - shift, 4)
                for parts, side in ((e_mine, core), (e_other, 1 - core)):
                    pieces.append((parts[shift].at[index], side, origin))
            for part, side, origin in pieces:
                small = pl.multiple_of(side * 256 + origin * 64, 64)
                start(part.at[pl.ds(256, 64)], out.at[layer, pl.ds(small, 64)], OUT, layer)
            for part, side in ((c_mine, core), (c_other, 1 - core)):
                start(part.at[:, index], up.at[layer, pl.ds(side * 8, 8)], IN, layer)
            for part, side, origin in pieces:
                large = pl.multiple_of(side * 1024 + origin * 256, 256)
                start(part.at[pl.ds(0, 256)], down.at[layer, pl.ds(large, 256)], DOWN, layer)
            for part, side, origin in pieces:
                small = pl.multiple_of(side * 256 + origin * 64, 64)
                start(part.at[pl.ds(320, 64)], dec.at[layer, pl.ds(small, 64)], DEC, layer)

    start(tok_all, tok, TOK, 0)


def roll_kernel(*refs):
    (place_ref, gains_ref, heads_ref, dec_gain_ref, tok_gain_ref), refs = refs[:5], refs[5:]
    blocks, refs = refs[:5], refs[5:]
    own, refs = refs[:5], refs[5:]
    tok_all, refs = refs[0], refs[1:]
    a_mine, a_other, refs = refs[:3], refs[3:6], refs[6:]
    c_mine, c_other, refs = refs[0], refs[1], refs[2:]
    e_mine, e_other, refs = refs[:4], refs[4:8], refs[8:]
    pred_ref, refs = refs[0], refs[1:]
    slots, rows_ref, sems = refs[:6], refs[6], refs[7]
    section, tile = place_ref[0], place_ref[1]
    start_weights(section, tile, own, tok_all, a_mine, a_other, c_mine, c_other, e_mine, e_other, slots, sems)

    def ready(kind, layer):
        place = slots[kind] if kind == TOK else slots[kind].at[layer]
        pltpu.make_async_copy(place, place, sems.at[kind, layer]).wait()

    column = tile // 2 % 4
    for index, block in enumerate(blocks):
        for shift in range(4):
            first = index * 128 + lax.rem(column + 4 - shift, 4) * 32
            rows_ref[pl.ds(pl.multiple_of(first, 32), 32), :] = block[shift]
    window = (2 * HALO + 1) * TOK_DEV
    first = pl.multiple_of((tile % 8 + 16 - HALO) * TOK_DEV, TOK_DEV)
    stream = rows_ref[pl.ds(first, window), :].astype(F32)

    row = lax.broadcasted_iota(jnp.int32, (256, 256), 0) // HEAD_DIM
    col = lax.broadcasted_iota(jnp.int32, (256, 256), 1) // HEAD_DIM
    pool = jnp.where(row == col, 1.0 / HEAD_DIM, 0.0).astype(BF16)

    for step in range(ROLL * LAYERS):
        frame, layer = step // LAYERS, step % LAYERS
        halo = HALO - step
        keys = (2 * halo + 1) * TOK_DEV
        rows = keys - 2 * TOK_DEV
        own_rows = slice(TOK_DEV, TOK_DEV + rows)
        normed = rms_scale(stream, gains_ref[layer : layer + 1, :]).astype(BF16)
        if frame == 0:
            ready(QKV, layer)
        projected = dot(normed, slots[QKV][layer])
        queries = head_scale(projected[own_rows, :WIDTH], heads_ref[layer : layer + 1, :], pool)
        key_rows = head_scale(
            projected[:, WIDTH : 2 * WIDTH], heads_ref[LAYERS + layer : LAYERS + layer + 1, :], pool
        )
        value_rows = projected[:, 2 * WIDTH :].astype(BF16)
        blended = []
        for start in range(0, rows, 96):
            count = min(96, rows - start)
            near = near_mask((tile - halo) * TOK_DEV + start, count, count + 32)
            spread = slice(start, start + count + 32)
            blended.append(
                attention(queries[start : start + count], key_rows[spread], value_rows[spread], near)
            )
        blended = jnp.concatenate(blended, axis=0)
        if frame == 0:
            ready(OUT, layer)
        attended = stream[own_rows] + dot(blended, slots[OUT][layer])
        normed_ff = rms_scale(attended, gains_ref[LAYERS + layer : LAYERS + layer + 1, :])
        if frame == 0:
            ready(IN, layer)
        up = slots[IN][layer].reshape(WIDTH, 4 * WIDTH)
        hidden = jax.nn.gelu(dot(normed_ff.astype(BF16), up)).astype(BF16)
        if frame == 0:
            ready(DOWN, layer)
        stream = attended + dot(hidden, slots[DOWN][layer])
        if layer == LAYERS - 1:
            normed_dec = rms_scale(stream, dec_gain_ref[...]).astype(BF16)
            if frame == 0:
                ready(TOK, 0)
            upcoming = jnp.zeros((rows, WIDTH), F32)
            middle = (rows - TOK_DEV) // 2
            for part in range(SECTIONS):
                if frame == 0:
                    ready(DEC, part)
                predicted = jnp.tanh(dot(normed_dec, slots[DEC][part])).astype(BF16)
                pred_ref[frame, part] = predicted[middle : middle + TOK_DEV]
                if frame + 1 < ROLL:
                    upcoming += dot(predicted, slots[TOK][part * 512 : part * 512 + 512])
            if frame + 1 < ROLL:
                stream = rms_scale(upcoming, tok_gain_ref[...]).astype(BF16).astype(F32)


def roll(place, gains, head_gains, dec_gain, tok_gain, blocks, weights):
    vmem = pl.BlockSpec(memory_space=pltpu.VMEM)
    return pl.pallas_call(
        roll_kernel,
        out_shape=jax.ShapeDtypeStruct((ROLL, SECTIONS, TOK_DEV, 512), BF16),
        in_specs=[pl.BlockSpec(memory_space=pltpu.SMEM)]
        + [vmem] * 9
        + [pl.BlockSpec(memory_space=pl.ANY)] * len(weights),
        out_specs=vmem,
        scratch_shapes=[
            pltpu.VMEM((LAYERS, 512, 1536), BF16),
            pltpu.VMEM((LAYERS, 512, 512), BF16),
            pltpu.VMEM((LAYERS, 16, 32, 2048), BF16),
            pltpu.VMEM((LAYERS, 2048, 512), BF16),
            pltpu.VMEM((LAYERS, 512, 512), BF16),
            pltpu.VMEM((2048, 512), BF16),
            pltpu.VMEM((640, WIDTH), BF16),
            pltpu.SemaphoreType.DMA((6, 4)),
        ],
        compiler_params=pltpu.CompilerParams(vmem_limit_bytes=56 * 1024 * 1024),
        name="roll",
    )(place, gains, head_gains, dec_gain, tok_gain, *blocks, *weights)


def scatter_kernel(points_ref, tok_gain_ref, tok_ref, out_ref):
    turned = jnp.transpose(points_ref[...].astype(F32))
    senders = turned.shape[1]
    cell_ids = lax.broadcasted_iota(jnp.int32, (64, senders), 0).astype(F32)
    voxel_ids = (lax.broadcasted_iota(jnp.int32, (128, senders), 0) % 64).astype(F32)
    totals = jnp.zeros((CHANNELS * 64, 128), F32)
    for slot in range(SLOTS):
        cell = turned[64 + slot : 65 + slot, :]
        voxel = turned[72 + slot : 73 + slot, :]
        here = cell_ids == cell
        picked = jnp.where(voxel_ids == voxel, 1.0, 0.0).astype(BF16)
        weighted = jnp.concatenate(
            [
                jnp.where(here, turned[slot * CHANNELS + e : slot * CHANNELS + e + 1, :], 0.0)
                for e in range(CHANNELS)
            ],
            axis=0,
        ).astype(BF16)
        totals = totals + dot_t(weighted, picked)
    low = low_lanes((TOK_DEV, 128))
    columns = []
    for section in range(SECTIONS):
        for e in range(0, CHANNELS, 2):
            first = e * 64 + section * TOK_DEV
            second = first + 64
            columns.append(
                jnp.where(low, totals[first : first + TOK_DEV], totals[second : second + TOK_DEV])
            )
    grid = jnp.concatenate(columns, axis=1).astype(BF16)
    out_ref[...] = rms_scale(dot(grid, tok_ref[...]), tok_gain_ref[...]).astype(BF16)


def scatter(points, tok_gain, tok_all):
    return pl.pallas_call(
        scatter_kernel,
        out_shape=jax.ShapeDtypeStruct((TOK_DEV, WIDTH), BF16),
        in_specs=[pl.BlockSpec(memory_space=pltpu.VMEM)] * 3,
        out_specs=pl.BlockSpec(memory_space=pltpu.VMEM),
        compiler_params=pltpu.CompilerParams(vmem_limit_bytes=32 * 1024 * 1024),
        name="scatter",
    )(points, tok_gain, tok_all)


def tile_of(z, y, core):
    return (z * 4 + y) * 2 + core


def places():
    return [(z, y, core) for z in range(8) for y in range(4) for core in range(2)]


def sibling(block):
    return lax.ppermute(block, "tok", [(i, i ^ 1) for i in range(TILES)])


def along_x(block, shift):
    return lax.ppermute(block, "segment", [(i, (i + shift) % SECTIONS) for i in range(SECTIONS)])


def along_y(block, shift):
    route = [(tile_of(z, y, core), tile_of(z, (y + shift) % 4, core)) for z, y, core in places()]
    return lax.ppermute(block, "tok", route)


def along_z(block, shift):
    route = [
        (tile_of(z, y, core), tile_of(z + shift, y, core))
        for z, y, core in places()
        if 0 <= z + shift < 8
    ]
    return lax.ppermute(block, "tok", route)


def along_z_all(block):
    groups = [[tile_of(z, y, core) for z in range(8)] for y in range(4) for core in range(2)]
    return lax.all_gather(block, "tok", axis_index_groups=groups)


def rows_of(weight, first, count):
    return lax.dynamic_slice_in_dim(weight, first, count, 0)


def gather_weights(qkv, out, up, down, dec):
    tile = lax.axis_index("tok")
    core, y, z = tile % 2, tile // 2 % 4, tile // 8
    c_piece = rows_of(up, core * 256 + z * 32, 32)
    c_mine = along_z_all(jnp.stack([along_x(c_piece, shift) for shift in (1, 2, 3)]))
    e_piece = jnp.concatenate(
        [
            rows_of(down, core * 1024 + y * 256, 256),
            rows_of(out, core * 256 + y * 64, 64),
            rows_of(dec, core * 256 + y * 64, 64),
        ]
    )
    e_own = jnp.stack([along_x(e_piece, shift) for shift in (1, 2, 3)])
    e_mine = [e_own] + [along_y(e_own, shift) for shift in (1, 2, 3)]
    a_piece = rows_of(qkv, core * 256, 256)
    a_piece, _ = lax.optimization_barrier((a_piece, e_own))
    a_mine = [along_x(a_piece, shift) for shift in (1, 2, 3)]
    return (
        a_mine
        + [sibling(part) for part in a_mine]
        + [c_mine, sibling(c_mine)]
        + e_mine
        + [sibling(part) for part in e_mine]
    )


def with_halo(block):
    core = lax.axis_index("tok") % 2
    other = sibling(block)
    pair = jnp.where(
        core == 0, jnp.concatenate([block, other]), jnp.concatenate([other, block])
    )
    own = jnp.stack([pair] + [along_y(pair, shift) for shift in (1, 2, 3)])
    return [own if shift == 0 else along_z(own, shift) for shift in (2, 1, 0, -1, -2)]


def send_points(point_feats, point_voxel, send_counts):
    feats = point_feats.reshape(SECTIONS * TILES, SLOTS * CHANNELS)
    voxel = point_voxel.reshape(SECTIONS * TILES, SLOTS)
    counts = send_counts.reshape(SECTIONS * TILES, 1)
    live = jnp.arange(SLOTS)[None, :] < counts
    cell = jnp.where(live, voxel // 64 % SECTIONS * TOK_DEV + voxel // 256, -1).astype(BF16)
    inner = (voxel % 64).astype(BF16)
    message = jnp.concatenate(
        [feats, cell, inner, jnp.zeros((SECTIONS * TILES, 48), BF16)], axis=1
    )
    return lax.all_to_all(message, ("segment", "tok"), split_axis=0, concat_axis=0, tiled=True)


def local(
    point_feats,
    point_voxel,
    send_counts,
    tok_weight,
    tok_gain,
    dec_weight,
    dec_gain,
    attn_gain,
    mlp_gain,
    query_gain,
    key_gain,
    qkv_weight,
    out_weight,
    in_weight,
    down_weight,
):
    place = jnp.stack([lax.axis_index("segment"), lax.axis_index("tok")]).astype(jnp.int32)
    tok_all = lax.all_gather(tok_weight, "segment", tiled=True)
    weights = gather_weights(qkv_weight[0], out_weight[0], in_weight[0], down_weight[0], dec_weight)
    own = [qkv_weight[0], out_weight[0], in_weight.reshape(16, 32, 2048), down_weight[0], dec_weight]
    points = send_points(point_feats, point_voxel, send_counts)
    own_gains = jnp.concatenate([attn_gain, mlp_gain, query_gain, key_gain], axis=1)
    all_gains = lax.all_to_all(
        jnp.broadcast_to(own_gains, (SECTIONS, own_gains.shape[1])),
        "segment",
        split_axis=0,
        concat_axis=0,
        tiled=True,
    )
    gains = jnp.concatenate([all_gains[:, :512], all_gains[:, 512:1024]], axis=0)
    head_gains = jnp.concatenate(
        [
            jnp.tile(all_gains[:, 1024:1088], (1, HEADS)) * 0.125,
            jnp.tile(all_gains[:, 1088:], (1, HEADS)),
        ],
        axis=0,
    )
    blocks = with_halo(scatter(points, tok_gain[None], tok_all))
    made = roll(
        place,
        gains,
        head_gains,
        dec_gain[None],
        tok_gain[None],
        blocks,
        own + [tok_all] + weights,
    )
    return lax.all_to_all(made, "segment", split_axis=1, concat_axis=1, tiled=True)


def solution(mesh):
    return jax.shard_map(
        local,
        mesh=mesh,
        in_specs=(
            P(None, ("segment", "tok"), None, None, None),
            P(None, ("segment", "tok"), None, None),
            P(None, ("segment", "tok"), None),
            P("segment", None),
            P(),
            P(None, "segment"),
            P(),
            P("segment", None),
            P("segment", None),
            P("segment", None),
            P("segment", None),
            P("segment", None, None),
            P("segment", None, None),
            P("segment", None, None),
            P("segment", None, None),
        ),
        out_specs=P(None, None, "tok", "segment"),
        check_vma=False,
    )
```

```python
import functools

import jax
import jax.numpy as jnp
from jax import lax
from jax.experimental import pallas as pl
from jax.experimental.pallas import tpu as pltpu
from jax.sharding import PartitionSpec as P

LAYERS = 4
ROLL = 3
TOK_DEV = 16
TILES = 64
TOKENS = TILES * TOK_DEV
WIDTH = 512
HEADS = 8
HEAD_DIM = 64
SECTIONS = 4
SLOTS = 8
CHANNELS = 8
HALO = ROLL * LAYERS
EPSILON = 1e-06
GROUP = 4
BLOCK = 96

F32 = jnp.float32
BF16 = jnp.bfloat16


def rms_scale(tensor, factor):
    return tensor * lax.rsqrt(jnp.mean(tensor * tensor, axis=-1, keepdims=True) + EPSILON) * factor


def dot(left, right):
    return jnp.dot(left, right, preferred_element_type=F32)


def dot_t(left, right):
    return lax.dot_general(left, right, (((1,), (1,)), ((), ())), preferred_element_type=F32)


def low_lanes(shape):
    return lax.broadcasted_iota(jnp.int32, shape, 1) % 128 < HEAD_DIM


def head_scale(tensor, factor, pool):
    parts = []
    for start in range(0, WIDTH, 256):
        part = tensor[:, start : start + 256]
        mean = dot((part * part).astype(BF16), pool)
        parts.append(part * lax.rsqrt(mean + EPSILON))
    return (jnp.concatenate(parts, axis=1) * factor).astype(BF16)


def lane_head(shape):
    return lax.broadcasted_iota(jnp.int32, shape, 1) // HEAD_DIM


def attention(queries, key_rows, value_rows, first_position):
    width = GROUP * HEAD_DIM
    todo = []
    for start in range(0, queries.shape[0], BLOCK):
        rows = min(BLOCK, queries.shape[0] - start)
        head = lane_head((rows, width))
        near = near_mask(first_position + start, rows, rows + 2 * TOK_DEV)
        for first in range(0, WIDTH, width):
            cols = slice(first, first + width)
            spread = slice(start, start + rows + 2 * TOK_DEV)
            own = queries[start : start + rows, cols]
            stacked = jnp.concatenate(
                [jnp.where(head == h, own, jnp.zeros_like(own)) for h in range(GROUP)], axis=0
            )
            todo.append((rows, head, near, spread, cols, dot_t(stacked, key_rows[spread, cols])))
    mixed = []
    for rows, head, near, spread, cols, scores in todo:
        weights = jnp.where(near, jnp.exp(scores), 0.0)
        total = jnp.maximum(jnp.sum(weights, axis=-1, keepdims=True), 1e-30)
        mixed.append(dot((weights * (1.0 / total)).astype(BF16), value_rows[spread, cols]))
    parts = []
    for (rows, head, *_), result in zip(todo, mixed):
        part = result[:rows]
        for h in range(1, GROUP):
            part = jnp.where(head == h, result[h * rows : (h + 1) * rows], part)
        parts.append(part)
    per = WIDTH // width
    strips = [jnp.concatenate(parts[i : i + per], axis=1) for i in range(0, len(parts), per)]
    return jnp.concatenate(strips, axis=0).astype(BF16)


def near_mask(first_position, rows, keys):
    query = lax.broadcasted_iota(jnp.int32, (GROUP * rows, keys), 0) % rows + TOK_DEV
    key = lax.broadcasted_iota(jnp.int32, (GROUP * rows, keys), 1)
    position = first_position + key
    return (jnp.abs(query - key) <= TOK_DEV) & (position >= 0) & (position < TOKENS)


QKV, OUT, IN, DOWN, DEC, TOK = range(6)


def start_weights(section, tile, own, t, a, c, d, o, slots, sems):
    core = tile % 2
    column = tile // 2 % 4
    qkv, out, up, down, dec, tok = slots

    def start(source, target, kind, layer):
        pltpu.make_async_copy(source, target, sems.at[kind, layer]).start()

    for layer in range(LAYERS):
        behind = lax.rem(section + LAYERS - layer, LAYERS)

        @pl.when(behind == 0)
        def _():
            for kind in (QKV, OUT, IN, DOWN, DEC, TOK):
                start(own[kind], slots[kind].at[layer], kind, layer)

        for source, step in enumerate((1, 3, 2)):

            @pl.when(behind == step)
            def _():
                for which, side in ((0, core), (1, 1 - core)):
                    half = pl.ds(pl.multiple_of(side * 256, 256), 256)
                    start(a[source][which], qkv.at[layer, half], QKV, layer)
                    start(t[which].at[source, pl.ds(0, 256)], tok.at[layer, half], TOK, layer)

        @pl.when(behind != 0)
        def _():
            index = jnp.maximum(behind - 1, 0)
            for which, side in ((0, core), (1, 1 - core)):
                half = pl.ds(side * 8, 8)
                start(o[which].at[:, index, pl.ds(0, 32)], out.at[layer, half], OUT, layer)
                start(c[which].at[:, index], up.at[layer, half], IN, layer)
                for source, shift in enumerate((0, 1, 3, 2)):
                    origin = lax.rem(column + 4 - shift, 4)
                    quarter = pl.ds(pl.multiple_of(side * 1024 + origin * 256, 256), 256)
                    start(d[source][which].at[index], down.at[layer, quarter], DOWN, layer)
                start(o[which].at[:, index, pl.ds(32, 32)], dec.at[layer, half], DEC, layer)


def roll_kernel(*refs):
    (place_ref, gains_ref, dec_gain_ref, tok_gain_ref), refs = refs[:4], refs[4:]
    blocks, refs = refs[:5], refs[5:]
    own, refs = refs[:6], refs[6:]
    pairs, refs = [refs[i : i + 2] for i in range(0, 20, 2)], refs[20:]
    t, a, c, d, o = pairs[0], pairs[1:4], pairs[4], pairs[5:9], pairs[9]
    pred_ref, refs = refs[0], refs[1:]
    slots, rows_ref, sems = refs[:6], refs[6], refs[7]
    section, tile = place_ref[0], place_ref[1]
    start_weights(section, tile, own, t, a, c, d, o, slots, sems)

    def ready(kind, layer):
        place = slots[kind].at[layer]
        pltpu.make_async_copy(place, place, sems.at[kind, layer]).wait()

    for index, block in enumerate(blocks):
        for apart in range(8):
            first = index * 128 + (tile % 8 ^ apart) * TOK_DEV
            rows_ref[pl.ds(pl.multiple_of(first, TOK_DEV), TOK_DEV), :] = block[apart]
    window = (2 * HALO + 1) * TOK_DEV
    first = pl.multiple_of((tile % 8 + 16 - HALO) * TOK_DEV, TOK_DEV)
    stream = rows_ref[pl.ds(first, window), :].astype(F32)

    row = lax.broadcasted_iota(jnp.int32, (256, 256), 0) // HEAD_DIM
    col = lax.broadcasted_iota(jnp.int32, (256, 256), 1) // HEAD_DIM
    pool = jnp.where(row == col, 1.0 / HEAD_DIM, 0.0).astype(BF16)

    for step in range(ROLL * LAYERS):
        frame, layer = step // LAYERS, step % LAYERS
        halo = HALO - step
        keys = (2 * halo + 1) * TOK_DEV
        rows = keys - 2 * TOK_DEV
        own_rows = slice(TOK_DEV, TOK_DEV + rows)
        gain = gains_ref[pl.ds(lax.rem(section + LAYERS - layer, LAYERS), 1), :]
        normed = rms_scale(stream, gain[:, :512]).astype(BF16)
        if frame == 0:
            ready(QKV, layer)
        projected = dot(normed, slots[QKV][layer])
        queries = head_scale(projected[own_rows, :WIDTH], gain[:, 1024:1536], pool)
        key_rows = head_scale(projected[:, WIDTH : 2 * WIDTH], gain[:, 1536:], pool)
        value_rows = projected[:, 2 * WIDTH :].astype(BF16)
        blended = attention(queries, key_rows, value_rows, (tile - halo) * TOK_DEV)
        if frame == 0:
            ready(OUT, layer)
        attended = stream[own_rows] + dot(blended, slots[OUT][layer].reshape(WIDTH, WIDTH))
        normed_ff = rms_scale(attended, gain[:, 512:1024])
        if frame == 0:
            ready(IN, layer)
        up = slots[IN][layer].reshape(WIDTH, 4 * WIDTH)
        hidden = jax.nn.gelu(dot(normed_ff.astype(BF16), up)).astype(BF16)
        if frame == 0:
            ready(DOWN, layer)
        stream = attended + dot(hidden, slots[DOWN][layer])
        if layer == LAYERS - 1:
            normed_dec = rms_scale(stream, dec_gain_ref[...]).astype(BF16)
            upcoming = jnp.zeros((rows, WIDTH), F32)
            middle = (rows - TOK_DEV) // 2
            for part in range(SECTIONS):
                if frame == 0:
                    ready(DEC, part)
                    ready(TOK, part)
                predicted = jnp.tanh(dot(normed_dec, slots[DEC][part].reshape(WIDTH, WIDTH))).astype(BF16)
                pred_ref[frame, part] = predicted[middle : middle + TOK_DEV]
                if frame + 1 < ROLL:
                    upcoming += dot(predicted, slots[TOK][part])
            if frame + 1 < ROLL:
                stream = rms_scale(upcoming, tok_gain_ref[...]).astype(BF16).astype(F32)


def roll(place, gains, dec_gain, tok_gain, blocks, weights):
    vmem = pl.BlockSpec(memory_space=pltpu.VMEM)
    return pl.pallas_call(
        roll_kernel,
        out_shape=jax.ShapeDtypeStruct((ROLL, SECTIONS, TOK_DEV, 512), BF16),
        in_specs=[pl.BlockSpec(memory_space=pltpu.SMEM)]
        + [vmem] * 8
        + [pl.BlockSpec(memory_space=pl.ANY)] * len(weights),
        out_specs=vmem,
        scratch_shapes=[
            pltpu.VMEM((LAYERS, 512, 1536), BF16),
            pltpu.VMEM((LAYERS, 16, 32, 512), BF16),
            pltpu.VMEM((LAYERS, 16, 32, 2048), BF16),
            pltpu.VMEM((LAYERS, 2048, 512), BF16),
            pltpu.VMEM((LAYERS, 16, 32, 512), BF16),
            pltpu.VMEM((LAYERS, 512, 512), BF16),
            pltpu.VMEM((640, WIDTH), BF16),
            pltpu.SemaphoreType.DMA((6, 4)),
        ],
        compiler_params=pltpu.CompilerParams(vmem_limit_bytes=56 * 1024 * 1024),
        name="roll",
    )(place, gains, dec_gain, tok_gain, *blocks, *weights)


def scatter_kernel(place_ref, points_ref, tok_gain_ref, own_ref, mine_ref, other_ref, out_ref, grid_ref):
    turned = jnp.transpose(points_ref[...].astype(F32))
    senders = turned.shape[1]
    cell_ids = lax.broadcasted_iota(jnp.int32, (64, senders), 0).astype(F32)
    voxel_ids = (lax.broadcasted_iota(jnp.int32, (128, senders), 0) % 64).astype(F32)
    totals = jnp.zeros((CHANNELS * 64, 128), F32)
    for slot in range(SLOTS):
        cell = turned[64 + slot : 65 + slot, :]
        voxel = turned[72 + slot : 73 + slot, :]
        here = cell_ids == cell
        picked = jnp.where(voxel_ids == voxel, 1.0, 0.0).astype(BF16)
        weighted = jnp.concatenate(
            [
                jnp.where(here, turned[slot * CHANNELS + e : slot * CHANNELS + e + 1, :], 0.0)
                for e in range(CHANNELS)
            ],
            axis=0,
        ).astype(BF16)
        totals = totals + dot_t(weighted, picked)
    low = low_lanes((TOK_DEV, 128))
    for section in range(SECTIONS):
        for side in range(2):
            columns = []
            for e in range(4 * side, 4 * side + 4, 2):
                first = e * 64 + section * TOK_DEV
                second = first + 64
                columns.append(
                    jnp.where(low, totals[first : first + TOK_DEV], totals[second : second + TOK_DEV])
                )
            grid_ref[section, side] = jnp.concatenate(columns, axis=1).astype(BF16)
    here, core = place_ref[0], place_ref[1] % 2
    summed = dot(grid_ref[here, 0], own_ref[:256]) + dot(grid_ref[here, 1], own_ref[256:])
    for index, step in enumerate((1, 3, 2)):
        behind = lax.rem(here + SECTIONS - step, SECTIONS)
        summed += dot(grid_ref[behind, core], mine_ref[index, :256])
        summed += dot(grid_ref[behind, 1 - core], other_ref[index, :256])
    out_ref[...] = rms_scale(summed, tok_gain_ref[...]).astype(BF16)


def scatter(place, points, tok_gain, own, mine, other):
    return pl.pallas_call(
        scatter_kernel,
        out_shape=jax.ShapeDtypeStruct((TOK_DEV, WIDTH), BF16),
        in_specs=[pl.BlockSpec(memory_space=pltpu.SMEM)] + [pl.BlockSpec(memory_space=pltpu.VMEM)] * 5,
        out_specs=pl.BlockSpec(memory_space=pltpu.VMEM),
        scratch_shapes=[pltpu.VMEM((SECTIONS, 2, TOK_DEV, 256), BF16)],
        compiler_params=pltpu.CompilerParams(vmem_limit_bytes=32 * 1024 * 1024),
        name="scatter",
    )(place, points, tok_gain, own, mine, other)


def tile_of(z, y, core):
    return (z * 4 + y) * 2 + core


def places():
    return [(z, y, core) for z in range(8) for y in range(4) for core in range(2)]


def sibling(block):
    return lax.ppermute(block, "tok", [(i, i ^ 1) for i in range(TILES)])


def along_x(block, shift):
    return lax.ppermute(block, "segment", [(i, (i + shift) % SECTIONS) for i in range(SECTIONS)])


def along_y(block, shift):
    route = [(tile_of(z, y, core), tile_of(z, (y + shift) % 4, core)) for z, y, core in places()]
    return lax.ppermute(block, "tok", route)


def along_z_all(block):
    groups = [[tile_of(z, y, core) for z in range(8)] for y in range(4) for core in range(2)]
    return lax.all_gather(block, "tok", axis_index_groups=groups)


def rows_of(weight, first, count):
    return lax.dynamic_slice_in_dim(weight, first, count, 0)


def together(*blocks):
    return lax.optimization_barrier(blocks)


def along_z(block, shift):
    route = [
        (tile_of(z, y, core), tile_of(z + shift, y, core))
        for z, y, core in places()
        if 0 <= z + shift < 8
    ]
    return lax.ppermute(block, "tok", route)


def row_of_tiles(block):
    blocks = block[None]
    for bit in (1, 2, 4):
        route = [(i, i ^ bit) for i in range(TILES)]
        blocks = jnp.concatenate([blocks, lax.ppermute(blocks, "tok", route)])
    return blocks


def both_ways(move, behind, ahead):
    middle = behind.shape[-1] // 2
    return jnp.concatenate([move(behind[..., :middle], 1), move(ahead[..., middle:], 3)], axis=-1)


def pack_gains(gains):
    high = lax.reduce_precision(gains, 8, 7)
    rest = gains - high
    middle = lax.reduce_precision(rest, 8, 7)
    terms = jnp.concatenate([high, middle, rest - middle]).astype(BF16)
    return jnp.pad(terms, (0, 16 * 512 - terms.shape[0])).reshape(16, 512)


def unpack_gains(rows, count):
    terms = rows.reshape(-1, 16 * 512)[:, : 3 * count].reshape(-1, 3, count).astype(F32)
    return (terms[:, 0] + terms[:, 1]) + terms[:, 2]


def point_message(point_feats, point_voxel, send_counts):
    feats = point_feats.reshape(SECTIONS * TILES, SLOTS * CHANNELS)
    voxel = point_voxel.reshape(SECTIONS * TILES, SLOTS)
    counts = send_counts.reshape(SECTIONS * TILES, 1)
    live = jnp.arange(SLOTS)[None, :] < counts
    cell = jnp.where(live, voxel // 64 % SECTIONS * TOK_DEV + voxel // 256, -1).astype(BF16)
    inner = (voxel % 64).astype(BF16)
    return jnp.concatenate([feats, cell, inner, jnp.zeros((SECTIONS * TILES, 48), BF16)], axis=1)


def local(
    point_feats,
    point_voxel,
    send_counts,
    tok_weight,
    tok_gain,
    dec_weight,
    dec_gain,
    attn_gain,
    mlp_gain,
    query_gain,
    key_gain,
    qkv_weight,
    out_weight,
    in_weight,
    down_weight,
):
    place = jnp.stack([lax.axis_index("segment"), lax.axis_index("tok")]).astype(jnp.int32)
    tile = lax.axis_index("tok")
    core, y, z = tile % 2, tile // 2 % 4, tile // 8
    qkv, out, up, down = qkv_weight[0], out_weight[0], in_weight[0], down_weight[0]
    shifts = (1, 2, 3)

    c_piece = rows_of(up, core * 256 + z * 32, 32)
    e_piece = jnp.concatenate(
        [
            rows_of(down, core * 1024 + y * 256, 256),
            rows_of(out, core * 256 + z * 32, 32),
            rows_of(dec_weight, core * 256 + z * 32, 32),
        ]
    )
    own_gains = jnp.concatenate([attn_gain, mlp_gain, query_gain, key_gain], axis=1)[0]
    t_piece = jnp.concatenate([rows_of(tok_weight, core * 256, 256), pack_gains(own_gains)])
    message = point_message(point_feats, point_voxel, send_counts)

    c_own = jnp.stack([along_x(c_piece, shift) for shift in shifts])
    t_near = [along_x(t_piece, 1), along_x(t_piece, 3)]
    c_own, e_piece, message, *t_near = together(c_own, e_piece, message, *t_near)

    c_mine = along_z_all(c_own)
    e_own = jnp.stack([along_x(e_piece, shift) for shift in shifts])
    t_mine = jnp.stack(t_near + [both_ways(along_x, *t_near)])
    points = lax.all_to_all(message, ("segment", "tok"), split_axis=0, concat_axis=0, tiled=True)
    a_piece = rows_of(qkv, core * 256, 256)
    e_own, t_mine, points, a_piece = together(e_own, t_mine, points, a_piece)

    t_other = sibling(t_mine)
    d_own, o_mine = e_own[:, :256], along_z_all(e_own[:, 256:])
    d_near = [along_y(d_own, 1), along_y(d_own, 3)]
    a_near = [along_x(a_piece, 1), along_x(a_piece, 3)]
    entering = scatter(place, points, tok_gain[None], tok_weight, t_mine, t_other)
    tiles = row_of_tiles(entering)
    *near, c_mine, tiles, d_own, a_piece = together(
        *d_near, *a_near, c_mine, tiles, d_own, a_piece
    )
    far = [along_y(d_own, 2), along_x(a_piece, 2)]
    blocks = [tiles if shift == 0 else along_z(tiles, shift) for shift in (2, 1, 0, -1, -2)]
    c_other, d_other = sibling(c_mine), sibling(d_own)
    near, far, c_other, d_other, o_mine, blocks = lax.optimization_barrier(
        (near, far, c_other, d_other, o_mine, blocks)
    )
    d_far, a_far = far

    gains = unpack_gains(t_mine[:, 256:], own_gains.shape[0])
    gains = jnp.concatenate([own_gains[None], gains[:1], gains[2:], gains[1:2]])
    query_gains = jnp.tile(gains[:, 1024:1088] * 0.125, (1, HEADS))
    key_gains = jnp.tile(gains[:, 1088:], (1, HEADS))
    weights = [qkv, out.reshape(16, 32, 512), up.reshape(16, 32, 2048), down]
    weights += [dec_weight.reshape(16, 32, 512), tok_weight, t_mine, t_other]
    for part in (near[2], near[3], a_far):
        weights += [part, sibling(part)]
    weights += [c_mine, c_other, d_own, d_other]
    for part in (near[0], near[1], d_far, o_mine):
        weights += [part, sibling(part)]
    made = roll(
        place,
        jnp.concatenate([gains[:, :1024], query_gains, key_gains], axis=1),
        dec_gain[None],
        tok_gain[None],
        blocks,
        weights,
    )
    return lax.all_to_all(made, "segment", split_axis=1, concat_axis=1, tiled=True)


def solution(mesh):
    return jax.shard_map(
        local,
        mesh=mesh,
        in_specs=(
            P(None, ("segment", "tok"), None, None, None),
            P(None, ("segment", "tok"), None, None),
            P(None, ("segment", "tok"), None),
            P("segment", None),
            P(),
            P(None, "segment"),
            P(),
            P("segment", None),
            P("segment", None),
            P("segment", None),
            P("segment", None),
            P("segment", None, None),
            P("segment", None, None),
            P("segment", None, None),
            P("segment", None, None),
        ),
        out_specs=P(None, None, "tok", "segment"),
        check_vma=False,
    )
```

```python
import functools

import jax
import jax.numpy as jnp
from jax import lax
from jax.experimental import pallas as pl
from jax.experimental.pallas import tpu as pltpu
from jax.sharding import PartitionSpec as P

LAYERS = 4
ROLL = 3
TOK_DEV = 16
TILES = 64
TOKENS = TILES * TOK_DEV
WIDTH = 512
HEADS = 8
HEAD_DIM = 64
SECTIONS = 4
SLOTS = 8
CHANNELS = 8
HALO = ROLL * LAYERS
EPSILON = 1e-06
GROUP = 4
BLOCK = 96

F32 = jnp.float32
BF16 = jnp.bfloat16


def rms_scale(tensor, factor):
    return tensor * lax.rsqrt(jnp.mean(tensor * tensor, axis=-1, keepdims=True) + EPSILON) * factor


def dot(left, right):
    return jnp.dot(left, right, preferred_element_type=F32)


def dot_t(left, right):
    return lax.dot_general(left, right, (((1,), (1,)), ((), ())), preferred_element_type=F32)


def low_lanes(shape):
    return lax.broadcasted_iota(jnp.int32, shape, 1) % 128 < HEAD_DIM


def head_scale(tensor, factor, pool):
    parts = []
    for start in range(0, WIDTH, 256):
        part = tensor[:, start : start + 256]
        mean = dot((part * part).astype(BF16), pool)
        parts.append(part * lax.rsqrt(mean + EPSILON))
    return (jnp.concatenate(parts, axis=1) * factor).astype(BF16)


def lane_head(shape):
    return lax.broadcasted_iota(jnp.int32, shape, 1) // HEAD_DIM


def attention(queries, key_rows, value_rows, first_position):
    width = GROUP * HEAD_DIM
    todo = []
    for start in range(0, queries.shape[0], BLOCK):
        rows = min(BLOCK, queries.shape[0] - start)
        head = lane_head((rows, width))
        near = near_mask(first_position + start, rows, rows + 2 * TOK_DEV)
        for first in range(0, WIDTH, width):
            cols = slice(first, first + width)
            spread = slice(start, start + rows + 2 * TOK_DEV)
            own = queries[start : start + rows, cols]
            stacked = jnp.concatenate(
                [jnp.where(head == h, own, jnp.zeros_like(own)) for h in range(GROUP)], axis=0
            )
            todo.append((rows, head, near, spread, cols, dot_t(stacked, key_rows[spread, cols])))
    mixed = []
    for rows, head, near, spread, cols, scores in todo:
        weights = jnp.where(near, jnp.exp(scores), 0.0)
        total = jnp.maximum(jnp.sum(weights, axis=-1, keepdims=True), 1e-30)
        mixed.append(dot((weights * (1.0 / total)).astype(BF16), value_rows[spread, cols]))
    parts = []
    for (rows, head, *_), result in zip(todo, mixed):
        part = result[:rows]
        for h in range(1, GROUP):
            part = jnp.where(head == h, result[h * rows : (h + 1) * rows], part)
        parts.append(part)
    per = WIDTH // width
    strips = [jnp.concatenate(parts[i : i + per], axis=1) for i in range(0, len(parts), per)]
    return jnp.concatenate(strips, axis=0).astype(BF16)


def near_mask(first_position, rows, keys):
    query = lax.broadcasted_iota(jnp.int32, (GROUP * rows, keys), 0) % rows + TOK_DEV
    key = lax.broadcasted_iota(jnp.int32, (GROUP * rows, keys), 1)
    position = first_position + key
    return (jnp.abs(query - key) <= TOK_DEV) & (position >= 0) & (position < TOKENS)


QKV, OUT, IN, DOWN, DEC, TOK = range(6)


def start_weights(section, tile, own, t, a, c, d, slots, sems):
    core = tile % 2
    column = tile // 2 % 4
    qkv, out, up, down, dec, tok = slots

    def start(source, target, kind, layer):
        pltpu.make_async_copy(source, target, sems.at[kind, layer]).start()

    for layer in range(LAYERS):
        behind = lax.rem(section + LAYERS - layer, LAYERS)

        @pl.when(behind == 0)
        def _():
            for kind in (QKV, OUT, IN, DOWN, DEC, TOK):
                start(own[kind], slots[kind].at[layer], kind, layer)

        for source, step in enumerate((1, 3, 2)):

            @pl.when(behind == step)
            def _():
                for which, side in ((0, core), (1, 1 - core)):
                    half = pl.ds(pl.multiple_of(side * 256, 256), 256)
                    start(a[source][which].at[:, pl.ds(0, 1536)], qkv.at[layer, half], QKV, layer)
                    start(a[source][which].at[:, pl.ds(1536, 512)], dec.at[layer, half], DEC, layer)
                    start(t[which].at[source, pl.ds(0, 256)], tok.at[layer, half], TOK, layer)

        @pl.when(behind != 0)
        def _():
            index = jnp.maximum(behind - 1, 0)
            for which, side in ((0, core), (1, 1 - core)):
                start(c[which].at[:, index], up.at[layer, pl.ds(side * 8, 8)], IN, layer)
                for source, shift in enumerate((0, 1, 3, 2)):
                    origin = lax.rem(column + 4 - shift, 4)
                    small = pl.ds(pl.multiple_of(side * 256 + origin * 64, 64), 64)
                    large = pl.ds(pl.multiple_of(side * 1024 + origin * 256, 256), 256)
                    start(d[source][which].at[index, pl.ds(256, 64)], out.at[layer, small], OUT, layer)
                    start(d[source][which].at[index, pl.ds(0, 256)], down.at[layer, large], DOWN, layer)


def roll_kernel(*refs):
    (place_ref, gains_ref, dec_gain_ref, tok_gain_ref), refs = refs[:4], refs[4:]
    blocks, refs = refs[:5], refs[5:]
    own, refs = refs[:6], refs[6:]
    pairs, refs = [refs[i : i + 2] for i in range(0, 18, 2)], refs[18:]
    t, a, c, d = pairs[0], pairs[1:4], pairs[4], pairs[5:]
    pred_ref, refs = refs[0], refs[1:]
    slots, rows_ref, sems = refs[:6], refs[6], refs[7]
    section, tile = place_ref[0], place_ref[1]
    start_weights(section, tile, own, t, a, c, d, slots, sems)

    def ready(kind, layer):
        place = slots[kind].at[layer]
        pltpu.make_async_copy(place, place, sems.at[kind, layer]).wait()

    for index, block in enumerate(blocks):
        for apart in range(8):
            first = index * 128 + (tile % 8 ^ apart) * TOK_DEV
            rows_ref[pl.ds(pl.multiple_of(first, TOK_DEV), TOK_DEV), :] = block[apart]
    window = (2 * HALO + 1) * TOK_DEV
    first = pl.multiple_of((tile % 8 + 16 - HALO) * TOK_DEV, TOK_DEV)
    stream = rows_ref[pl.ds(first, window), :].astype(F32)

    row = lax.broadcasted_iota(jnp.int32, (256, 256), 0) // HEAD_DIM
    col = lax.broadcasted_iota(jnp.int32, (256, 256), 1) // HEAD_DIM
    pool = jnp.where(row == col, 1.0 / HEAD_DIM, 0.0).astype(BF16)

    for step in range(ROLL * LAYERS):
        frame, layer = step // LAYERS, step % LAYERS
        halo = HALO - step
        keys = (2 * halo + 1) * TOK_DEV
        rows = keys - 2 * TOK_DEV
        own_rows = slice(TOK_DEV, TOK_DEV + rows)
        gain = gains_ref[pl.ds(lax.rem(section + LAYERS - layer, LAYERS), 1), :]
        normed = rms_scale(stream, gain[:, :512]).astype(BF16)
        if frame == 0:
            ready(QKV, layer)
        projected = dot(normed, slots[QKV][layer])
        queries = head_scale(projected[own_rows, :WIDTH], gain[:, 1024:1536], pool)
        key_rows = head_scale(projected[:, WIDTH : 2 * WIDTH], gain[:, 1536:], pool)
        value_rows = projected[:, 2 * WIDTH :].astype(BF16)
        blended = attention(queries, key_rows, value_rows, (tile - halo) * TOK_DEV)
        if frame == 0:
            ready(OUT, layer)
        attended = stream[own_rows] + dot(blended, slots[OUT][layer])
        normed_ff = rms_scale(attended, gain[:, 512:1024])
        if frame == 0:
            ready(IN, layer)
        up = slots[IN][layer].reshape(WIDTH, 4 * WIDTH)
        hidden = jax.nn.gelu(dot(normed_ff.astype(BF16), up)).astype(BF16)
        if frame == 0:
            ready(DOWN, layer)
        stream = attended + dot(hidden, slots[DOWN][layer])
        if layer == LAYERS - 1:
            normed_dec = rms_scale(stream, dec_gain_ref[...]).astype(BF16)
            upcoming = jnp.zeros((rows, WIDTH), F32)
            middle = (rows - TOK_DEV) // 2
            for part in range(SECTIONS):
                if frame == 0:
                    ready(DEC, part)
                    ready(TOK, part)
                predicted = jnp.tanh(dot(normed_dec, slots[DEC][part])).astype(BF16)
                pred_ref[frame, part] = predicted[middle : middle + TOK_DEV]
                if frame + 1 < ROLL:
                    upcoming += dot(predicted, slots[TOK][part])
            if frame + 1 < ROLL:
                stream = rms_scale(upcoming, tok_gain_ref[...]).astype(BF16).astype(F32)


def roll(place, gains, dec_gain, tok_gain, blocks, weights):
    vmem = pl.BlockSpec(memory_space=pltpu.VMEM)
    return pl.pallas_call(
        roll_kernel,
        out_shape=jax.ShapeDtypeStruct((ROLL, SECTIONS, TOK_DEV, 512), BF16),
        in_specs=[pl.BlockSpec(memory_space=pltpu.SMEM)]
        + [vmem] * 8
        + [pl.BlockSpec(memory_space=pl.ANY)] * len(weights),
        out_specs=vmem,
        scratch_shapes=[
            pltpu.VMEM((LAYERS, 512, 1536), BF16),
            pltpu.VMEM((LAYERS, 512, 512), BF16),
            pltpu.VMEM((LAYERS, 16, 32, 2048), BF16),
            pltpu.VMEM((LAYERS, 2048, 512), BF16),
            pltpu.VMEM((LAYERS, 512, 512), BF16),
            pltpu.VMEM((LAYERS, 512, 512), BF16),
            pltpu.VMEM((640, WIDTH), BF16),
            pltpu.SemaphoreType.DMA((6, 4)),
        ],
        compiler_params=pltpu.CompilerParams(vmem_limit_bytes=56 * 1024 * 1024),
        name="roll",
    )(place, gains, dec_gain, tok_gain, *blocks, *weights)


def scatter_kernel(place_ref, points_ref, tok_gain_ref, own_ref, mine_ref, other_ref, out_ref, grid_ref):
    turned = jnp.transpose(points_ref[...].astype(F32))
    senders = turned.shape[1]
    cell_ids = lax.broadcasted_iota(jnp.int32, (64, senders), 0).astype(F32)
    voxel_ids = (lax.broadcasted_iota(jnp.int32, (128, senders), 0) % 64).astype(F32)
    totals = jnp.zeros((CHANNELS * 64, 128), F32)
    for slot in range(SLOTS):
        cell = turned[64 + slot : 65 + slot, :]
        voxel = turned[72 + slot : 73 + slot, :]
        here = cell_ids == cell
        picked = jnp.where(voxel_ids == voxel, 1.0, 0.0).astype(BF16)
        weighted = jnp.concatenate(
            [
                jnp.where(here, turned[slot * CHANNELS + e : slot * CHANNELS + e + 1, :], 0.0)
                for e in range(CHANNELS)
            ],
            axis=0,
        ).astype(BF16)
        totals = totals + dot_t(weighted, picked)
    low = low_lanes((TOK_DEV, 128))
    for section in range(SECTIONS):
        for side in range(2):
            columns = []
            for e in range(4 * side, 4 * side + 4, 2):
                first = e * 64 + section * TOK_DEV
                second = first + 64
                columns.append(
                    jnp.where(low, totals[first : first + TOK_DEV], totals[second : second + TOK_DEV])
                )
            grid_ref[section, side] = jnp.concatenate(columns, axis=1).astype(BF16)
    here, core = place_ref[0], place_ref[1] % 2
    summed = dot(grid_ref[here, 0], own_ref[:256]) + dot(grid_ref[here, 1], own_ref[256:])
    for index, step in enumerate((1, 3, 2)):
        behind = lax.rem(here + SECTIONS - step, SECTIONS)
        summed += dot(grid_ref[behind, core], mine_ref[index, :256])
        summed += dot(grid_ref[behind, 1 - core], other_ref[index, :256])
    out_ref[...] = rms_scale(summed, tok_gain_ref[...]).astype(BF16)


def scatter(place, points, tok_gain, own, mine, other):
    return pl.pallas_call(
        scatter_kernel,
        out_shape=jax.ShapeDtypeStruct((TOK_DEV, WIDTH), BF16),
        in_specs=[pl.BlockSpec(memory_space=pltpu.SMEM)] + [pl.BlockSpec(memory_space=pltpu.VMEM)] * 5,
        out_specs=pl.BlockSpec(memory_space=pltpu.VMEM),
        scratch_shapes=[pltpu.VMEM((SECTIONS, 2, TOK_DEV, 256), BF16)],
        compiler_params=pltpu.CompilerParams(vmem_limit_bytes=32 * 1024 * 1024),
        name="scatter",
    )(place, points, tok_gain, own, mine, other)


def tile_of(z, y, core):
    return (z * 4 + y) * 2 + core


def places():
    return [(z, y, core) for z in range(8) for y in range(4) for core in range(2)]


def sibling(block):
    return lax.ppermute(block, "tok", [(i, i ^ 1) for i in range(TILES)])


def along_x(block, shift):
    return lax.ppermute(block, "segment", [(i, (i + shift) % SECTIONS) for i in range(SECTIONS)])


def along_y(block, shift):
    route = [(tile_of(z, y, core), tile_of(z, (y + shift) % 4, core)) for z, y, core in places()]
    return lax.ppermute(block, "tok", route)


def along_z_all(block):
    groups = [[tile_of(z, y, core) for z in range(8)] for y in range(4) for core in range(2)]
    return lax.all_gather(block, "tok", axis_index_groups=groups)


def rows_of(weight, first, count):
    return lax.dynamic_slice_in_dim(weight, first, count, 0)


def together(*blocks):
    return lax.optimization_barrier(blocks)


def along_z(block, shift):
    route = [
        (tile_of(z, y, core), tile_of(z + shift, y, core))
        for z, y, core in places()
        if 0 <= z + shift < 8
    ]
    return lax.ppermute(block, "tok", route)


def row_of_tiles(block):
    blocks = block[None]
    for bit in (1, 2, 4):
        route = [(i, i ^ bit) for i in range(TILES)]
        blocks = jnp.concatenate([blocks, lax.ppermute(blocks, "tok", route)])
    return blocks


def both_ways(move, behind, ahead):
    middle = behind.shape[-1] // 2
    return jnp.concatenate([move(behind[..., :middle], 1), move(ahead[..., middle:], 3)], axis=-1)


def pack_gains(gains):
    high = lax.reduce_precision(gains, 8, 7)
    rest = gains - high
    middle = lax.reduce_precision(rest, 8, 7)
    terms = jnp.concatenate([high, middle, rest - middle]).astype(BF16)
    return jnp.pad(terms, (0, 16 * 512 - terms.shape[0])).reshape(16, 512)


def unpack_gains(rows, count):
    terms = rows.reshape(-1, 16 * 512)[:, : 3 * count].reshape(-1, 3, count).astype(F32)
    return (terms[:, 0] + terms[:, 1]) + terms[:, 2]


def point_message(point_feats, point_voxel, send_counts):
    feats = point_feats.reshape(SECTIONS * TILES, SLOTS * CHANNELS)
    voxel = point_voxel.reshape(SECTIONS * TILES, SLOTS)
    counts = send_counts.reshape(SECTIONS * TILES, 1)
    live = jnp.arange(SLOTS)[None, :] < counts
    cell = jnp.where(live, voxel // 64 % SECTIONS * TOK_DEV + voxel // 256, -1).astype(BF16)
    inner = (voxel % 64).astype(BF16)
    return jnp.concatenate([feats, cell, inner, jnp.zeros((SECTIONS * TILES, 48), BF16)], axis=1)


def local(
    point_feats,
    point_voxel,
    send_counts,
    tok_weight,
    tok_gain,
    dec_weight,
    dec_gain,
    attn_gain,
    mlp_gain,
    query_gain,
    key_gain,
    qkv_weight,
    out_weight,
    in_weight,
    down_weight,
):
    place = jnp.stack([lax.axis_index("segment"), lax.axis_index("tok")]).astype(jnp.int32)
    tile = lax.axis_index("tok")
    core, y, z = tile % 2, tile // 2 % 4, tile // 8
    qkv, out, up, down = qkv_weight[0], out_weight[0], in_weight[0], down_weight[0]
    shifts = (1, 2, 3)

    c_piece = rows_of(up, core * 256 + z * 32, 32)
    e_piece = jnp.concatenate(
        [
            rows_of(down, core * 1024 + y * 256, 256),
            rows_of(out, core * 256 + y * 64, 64),
        ]
    )
    own_gains = jnp.concatenate([attn_gain, mlp_gain, query_gain, key_gain], axis=1)[0]
    t_piece = jnp.concatenate([rows_of(tok_weight, core * 256, 256), pack_gains(own_gains)])
    message = point_message(point_feats, point_voxel, send_counts)

    c_own = jnp.stack([along_x(c_piece, shift) for shift in shifts])
    t_near = [along_x(t_piece, 1), along_x(t_piece, 3)]
    c_own, e_piece, message, *t_near = together(c_own, e_piece, message, *t_near)

    c_mine = along_z_all(c_own)
    e_own = jnp.stack([along_x(e_piece, shift) for shift in shifts])
    t_mine = jnp.stack(t_near + [both_ways(along_x, *t_near)])
    points = lax.all_to_all(message, ("segment", "tok"), split_axis=0, concat_axis=0, tiled=True)
    a_piece = jnp.concatenate(
        [rows_of(qkv, core * 256, 256), rows_of(dec_weight, core * 256, 256)], axis=1
    )
    e_own, t_mine, points, a_piece = together(e_own, t_mine, points, a_piece)

    t_other = sibling(t_mine)
    near = [along_y(e_own, 1), along_y(e_own, 3), along_x(a_piece, 1), along_x(a_piece, 3)]
    tiles = row_of_tiles(scatter(place, points, tok_gain[None], tok_weight, t_mine, t_other))
    near, c_mine, tiles, e_own, a_piece = lax.optimization_barrier(
        (near, c_mine, tiles, e_own, a_piece)
    )
    far = [along_y(e_own, 2), along_x(a_piece, 2)]
    blocks = [tiles if shift == 0 else along_z(tiles, shift) for shift in (2, 1, 0, -1, -2)]
    near, far, blocks = lax.optimization_barrier((near, far, blocks))

    gains = unpack_gains(t_mine[:, 256:], own_gains.shape[0])
    gains = jnp.concatenate([own_gains[None], gains[:1], gains[2:], gains[1:2]])
    query_gains = jnp.tile(gains[:, 1024:1088] * 0.125, (1, HEADS))
    key_gains = jnp.tile(gains[:, 1088:], (1, HEADS))
    weights = [qkv, out, up.reshape(16, 32, 2048), down, dec_weight, tok_weight, t_mine, t_other]
    for part in (near[2], near[3], far[1], c_mine, e_own, near[0], near[1], far[0]):
        weights += [part, sibling(part)]
    made = roll(
        place,
        jnp.concatenate([gains[:, :1024], query_gains, key_gains], axis=1),
        dec_gain[None],
        tok_gain[None],
        blocks,
        weights,
    )
    return lax.all_to_all(made, "segment", split_axis=1, concat_axis=1, tiled=True)


def solution(mesh):
    return jax.shard_map(
        local,
        mesh=mesh,
        in_specs=(
            P(None, ("segment", "tok"), None, None, None),
            P(None, ("segment", "tok"), None, None),
            P(None, ("segment", "tok"), None),
            P("segment", None),
            P(),
            P(None, "segment"),
            P(),
            P("segment", None),
            P("segment", None),
            P("segment", None),
            P("segment", None),
            P("segment", None, None),
            P("segment", None, None),
            P("segment", None, None),
            P("segment", None, None),
        ),
        out_specs=P(None, None, "tok", "segment"),
        check_vma=False,
    )
```

```python
import functools

import jax
import jax.numpy as jnp
from jax import lax
from jax.experimental import pallas as pl
from jax.experimental.pallas import tpu as pltpu
from jax.sharding import PartitionSpec as P

LAYERS = 4
ROLL = 3
TOK_DEV = 16
TILES = 64
TOKENS = TILES * TOK_DEV
WIDTH = 512
HEADS = 8
HEAD_DIM = 64
SECTIONS = 4
SLOTS = 8
CHANNELS = 8
HALO = ROLL * LAYERS
EPSILON = 1e-06
GROUP = 4
BLOCK = 96

F32 = jnp.float32
BF16 = jnp.bfloat16


def rms_scale(tensor, factor):
    return tensor * lax.rsqrt(jnp.mean(tensor * tensor, axis=-1, keepdims=True) + EPSILON) * factor


def dot(left, right):
    return jnp.dot(left, right, preferred_element_type=F32)


def dot_t(left, right):
    return lax.dot_general(left, right, (((1,), (1,)), ((), ())), preferred_element_type=F32)


def low_lanes(shape):
    return lax.broadcasted_iota(jnp.int32, shape, 1) % 128 < HEAD_DIM


def head_scale(tensor, factor, pool):
    parts = []
    for start in range(0, WIDTH, 256):
        part = tensor[:, start : start + 256]
        mean = dot((part * part).astype(BF16), pool)
        parts.append(part * lax.rsqrt(mean + EPSILON))
    return (jnp.concatenate(parts, axis=1) * factor).astype(BF16)


def lane_head(shape):
    return lax.broadcasted_iota(jnp.int32, shape, 1) // HEAD_DIM


def attention(queries, key_rows, value_rows, first_position):
    width = GROUP * HEAD_DIM
    todo = []
    for start in range(0, queries.shape[0], BLOCK):
        rows = min(BLOCK, queries.shape[0] - start)
        head = lane_head((rows, width))
        near = near_mask(first_position + start, rows, rows + 2 * TOK_DEV)
        for first in range(0, WIDTH, width):
            cols = slice(first, first + width)
            spread = slice(start, start + rows + 2 * TOK_DEV)
            own = queries[start : start + rows, cols]
            stacked = jnp.concatenate(
                [jnp.where(head == h, own, jnp.zeros_like(own)) for h in range(GROUP)], axis=0
            )
            todo.append((rows, head, near, spread, cols, dot_t(stacked, key_rows[spread, cols])))
    mixed = []
    for rows, head, near, spread, cols, scores in todo:
        weights = jnp.where(near, jnp.exp(scores), 0.0)
        total = jnp.maximum(jnp.sum(weights, axis=-1, keepdims=True), 1e-30)
        mixed.append(dot((weights * (1.0 / total)).astype(BF16), value_rows[spread, cols]))
    parts = []
    for (rows, head, *_), result in zip(todo, mixed):
        part = result[:rows]
        for h in range(1, GROUP):
            part = jnp.where(head == h, result[h * rows : (h + 1) * rows], part)
        parts.append(part)
    per = WIDTH // width
    strips = [jnp.concatenate(parts[i : i + per], axis=1) for i in range(0, len(parts), per)]
    return jnp.concatenate(strips, axis=0).astype(BF16)


def near_mask(first_position, rows, keys):
    query = lax.broadcasted_iota(jnp.int32, (GROUP * rows, keys), 0) % rows + TOK_DEV
    key = lax.broadcasted_iota(jnp.int32, (GROUP * rows, keys), 1)
    position = first_position + key
    return (jnp.abs(query - key) <= TOK_DEV) & (position >= 0) & (position < TOKENS)


QKV, OUT, IN, DOWN, DEC, TOK = range(6)


def start_weights(section, tile, own, t, a, c, d, slots, sems):
    core = tile % 2
    column = tile // 2 % 4
    qkv, _, _, down, _, tok = slots

    def start(source, target, kind, layer):
        pltpu.make_async_copy(source, target, sems.at[kind, layer]).start()

    for layer in range(LAYERS):
        behind = lax.rem(section + LAYERS - layer, LAYERS)

        @pl.when(behind == 0)
        def _():
            for kind in (QKV, OUT, IN, DOWN, DEC, TOK):
                start(own[kind], slots[kind].at[layer], kind, layer)

        for source, step in enumerate((1, 3, 2)):

            @pl.when(behind == step)
            def _():
                for which, side in ((0, core), (1, 1 - core)):
                    half = pl.ds(pl.multiple_of(side * 256, 256), 256)
                    start(a[source][which], qkv.at[layer, half], QKV, layer)
                    start(t[which].at[source, pl.ds(0, 256)], tok.at[layer, half], TOK, layer)

        @pl.when(behind != 0)
        def _():
            index = jnp.maximum(behind - 1, 0)
            for which, side in ((0, core), (1, 1 - core)):
                for kind, first, width in ((OUT, 2048, 512), (IN, 0, 2048), (DEC, 2560, 512)):
                    part = c[which].at[:, index, :, pl.ds(first, width)]
                    start(part, slots[kind].at[layer, pl.ds(side * 8, 8)], kind, layer)
                for source, shift in enumerate((0, 1, 3, 2)):
                    origin = lax.rem(column + 4 - shift, 4)
                    large = pl.ds(pl.multiple_of(side * 1024 + origin * 256, 256), 256)
                    start(d[source][which].at[index], down.at[layer, large], DOWN, layer)


def roll_kernel(*refs):
    (place_ref, gains_ref, dec_gain_ref, tok_gain_ref), refs = refs[:4], refs[4:]
    blocks, refs = refs[:5], refs[5:]
    own, refs = refs[:6], refs[6:]
    pairs, refs = [refs[i : i + 2] for i in range(0, 18, 2)], refs[18:]
    t, a, c, d = pairs[0], pairs[1:4], pairs[4], pairs[5:]
    pred_refs, refs = refs[:4], refs[4:]
    slots, rows_ref, pred_ref, sems = refs[:6], refs[6], refs[7], refs[8]
    section, tile = place_ref[0], place_ref[1]
    start_weights(section, tile, own, t, a, c, d, slots, sems)

    def ready(kind, layer):
        place = slots[kind].at[layer]
        pltpu.make_async_copy(place, place, sems.at[kind, layer]).wait()

    for index, block in enumerate(blocks):
        for apart in range(8):
            first = index * 128 + (tile % 8 ^ apart) * TOK_DEV
            rows_ref[pl.ds(pl.multiple_of(first, TOK_DEV), TOK_DEV), :] = block[apart]
    window = (2 * HALO + 1) * TOK_DEV
    first = pl.multiple_of((tile % 8 + 16 - HALO) * TOK_DEV, TOK_DEV)
    stream = rows_ref[pl.ds(first, window), :].astype(F32)

    row = lax.broadcasted_iota(jnp.int32, (256, 256), 0) // HEAD_DIM
    col = lax.broadcasted_iota(jnp.int32, (256, 256), 1) // HEAD_DIM
    pool = jnp.where(row == col, 1.0 / HEAD_DIM, 0.0).astype(BF16)

    for step in range(ROLL * LAYERS):
        frame, layer = step // LAYERS, step % LAYERS
        halo = HALO - step
        keys = (2 * halo + 1) * TOK_DEV
        rows = keys - 2 * TOK_DEV
        own_rows = slice(TOK_DEV, TOK_DEV + rows)
        gain = gains_ref[pl.ds(lax.rem(section + LAYERS - layer, LAYERS), 1), :]
        normed = rms_scale(stream, gain[:, :512]).astype(BF16)
        if frame == 0:
            ready(QKV, layer)
        projected = dot(normed, slots[QKV][layer])
        queries = head_scale(projected[own_rows, :WIDTH], gain[:, 1024:1536], pool)
        key_rows = head_scale(projected[:, WIDTH : 2 * WIDTH], gain[:, 1536:], pool)
        value_rows = projected[:, 2 * WIDTH :].astype(BF16)
        blended = attention(queries, key_rows, value_rows, (tile - halo) * TOK_DEV)
        if frame == 0:
            ready(OUT, layer)
        attended = stream[own_rows] + dot(blended, slots[OUT][layer].reshape(WIDTH, WIDTH))
        normed_ff = rms_scale(attended, gain[:, 512:1024])
        if frame == 0:
            ready(IN, layer)
        up = slots[IN][layer].reshape(WIDTH, 4 * WIDTH)
        hidden = jax.nn.gelu(dot(normed_ff.astype(BF16), up)).astype(BF16)
        if frame == 0:
            ready(DOWN, layer)
        stream = attended + dot(hidden, slots[DOWN][layer])
        if layer == LAYERS - 1:
            normed_dec = rms_scale(stream, dec_gain_ref[...]).astype(BF16)
            upcoming = jnp.zeros((rows, WIDTH), F32)
            middle = (rows - TOK_DEV) // 2
            for part in range(SECTIONS):
                if frame == 0:
                    ready(DEC, part)
                    ready(TOK, part)
                predicted = jnp.tanh(dot(normed_dec, slots[DEC][part].reshape(WIDTH, WIDTH))).astype(BF16)
                ahead = lax.rem(part + SECTIONS - section, SECTIONS)
                pred_ref[ahead, frame] = predicted[middle : middle + TOK_DEV]
                if frame + 1 < ROLL:
                    upcoming += dot(predicted, slots[TOK][part])
            if frame + 1 < ROLL:
                stream = rms_scale(upcoming, tok_gain_ref[...]).astype(BF16).astype(F32)
    for ahead in range(SECTIONS):
        pred_refs[ahead][...] = pred_ref[ahead]


def roll(place, gains, dec_gain, tok_gain, blocks, weights):
    vmem = pl.BlockSpec(memory_space=pltpu.VMEM)
    return pl.pallas_call(
        roll_kernel,
        out_shape=[jax.ShapeDtypeStruct((ROLL, TOK_DEV, 512), BF16)] * SECTIONS,
        in_specs=[pl.BlockSpec(memory_space=pltpu.SMEM)]
        + [vmem] * 8
        + [pl.BlockSpec(memory_space=pl.ANY)] * len(weights),
        out_specs=[vmem] * SECTIONS,
        scratch_shapes=[
            pltpu.VMEM((LAYERS, 512, 1536), BF16),
            pltpu.VMEM((LAYERS, 16, 32, 512), BF16),
            pltpu.VMEM((LAYERS, 16, 32, 2048), BF16),
            pltpu.VMEM((LAYERS, 2048, 512), BF16),
            pltpu.VMEM((LAYERS, 16, 32, 512), BF16),
            pltpu.VMEM((LAYERS, 512, 512), BF16),
            pltpu.VMEM((640, WIDTH), BF16),
            pltpu.VMEM((SECTIONS, ROLL, TOK_DEV, 512), BF16),
            pltpu.SemaphoreType.DMA((6, 4)),
        ],
        compiler_params=pltpu.CompilerParams(vmem_limit_bytes=56 * 1024 * 1024),
        name="roll",
    )(place, gains, dec_gain, tok_gain, *blocks, *weights)


def place_scenes_kernel(place_ref, *refs):
    for behind in range(SECTIONS):
        scene = lax.rem(place_ref[0] + SECTIONS - behind, SECTIONS)
        for frame in range(ROLL):
            refs[SECTIONS][frame, scene] = refs[behind][frame]


def place_scenes(place, parts):
    vmem = pl.BlockSpec(memory_space=pltpu.VMEM)
    return pl.pallas_call(
        place_scenes_kernel,
        out_shape=jax.ShapeDtypeStruct((ROLL, SECTIONS, TOK_DEV, 512), BF16),
        in_specs=[pl.BlockSpec(memory_space=pltpu.SMEM)] + [vmem] * SECTIONS,
        out_specs=vmem,
        name="place_scenes",
    )(place, *parts)


def scatter_kernel(place_ref, points_ref, tok_gain_ref, own_ref, mine_ref, other_ref, out_ref, grid_ref):
    turned = jnp.transpose(points_ref[...].astype(F32))
    senders = turned.shape[1]
    cell_ids = lax.broadcasted_iota(jnp.int32, (64, senders), 0).astype(F32)
    voxel_ids = (lax.broadcasted_iota(jnp.int32, (128, senders), 0) % 64).astype(F32)
    totals = jnp.zeros((CHANNELS * 64, 128), F32)
    for slot in range(SLOTS):
        cell = turned[64 + slot : 65 + slot, :]
        voxel = turned[72 + slot : 73 + slot, :]
        here = cell_ids == cell
        picked = jnp.where(voxel_ids == voxel, 1.0, 0.0).astype(BF16)
        weighted = jnp.concatenate(
            [
                jnp.where(here, turned[slot * CHANNELS + e : slot * CHANNELS + e + 1, :], 0.0)
                for e in range(CHANNELS)
            ],
            axis=0,
        ).astype(BF16)
        totals = totals + dot_t(weighted, picked)
    low = low_lanes((TOK_DEV, 128))
    for section in range(SECTIONS):
        for side in range(2):
            columns = []
            for e in range(4 * side, 4 * side + 4, 2):
                first = e * 64 + section * TOK_DEV
                second = first + 64
                columns.append(
                    jnp.where(low, totals[first : first + TOK_DEV], totals[second : second + TOK_DEV])
                )
            grid_ref[section, side] = jnp.concatenate(columns, axis=1).astype(BF16)
    here, core = place_ref[0], place_ref[1] % 2
    summed = dot(grid_ref[here, 0], own_ref[:256]) + dot(grid_ref[here, 1], own_ref[256:])
    for index, step in enumerate((1, 3, 2)):
        behind = lax.rem(here + SECTIONS - step, SECTIONS)
        summed += dot(grid_ref[behind, core], mine_ref[index, :256])
        summed += dot(grid_ref[behind, 1 - core], other_ref[index, :256])
    out_ref[...] = rms_scale(summed, tok_gain_ref[...]).astype(BF16)


def scatter(place, points, tok_gain, own, mine, other):
    return pl.pallas_call(
        scatter_kernel,
        out_shape=jax.ShapeDtypeStruct((TOK_DEV, WIDTH), BF16),
        in_specs=[pl.BlockSpec(memory_space=pltpu.SMEM)] + [pl.BlockSpec(memory_space=pltpu.VMEM)] * 5,
        out_specs=pl.BlockSpec(memory_space=pltpu.VMEM),
        scratch_shapes=[pltpu.VMEM((SECTIONS, 2, TOK_DEV, 256), BF16)],
        compiler_params=pltpu.CompilerParams(vmem_limit_bytes=32 * 1024 * 1024),
        name="scatter",
    )(place, points, tok_gain, own, mine, other)


def tile_of(z, y, core):
    return (z * 4 + y) * 2 + core


def places():
    return [(z, y, core) for z in range(8) for y in range(4) for core in range(2)]


def sibling(block):
    return lax.ppermute(block, "tok", [(i, i ^ 1) for i in range(TILES)])


def along_x(block, shift):
    return lax.ppermute(block, "segment", [(i, (i + shift) % SECTIONS) for i in range(SECTIONS)])


def along_y(block, shift):
    route = [(tile_of(z, y, core), tile_of(z, (y + shift) % 4, core)) for z, y, core in places()]
    return lax.ppermute(block, "tok", route)


def along_z_all(block):
    groups = [[tile_of(z, y, core) for z in range(8)] for y in range(4) for core in range(2)]
    return lax.all_gather(block, "tok", axis_index_groups=groups)


def rows_of(weight, first, count):
    return lax.dynamic_slice_in_dim(weight, first, count, 0)


def together(*blocks):
    return lax.optimization_barrier(blocks)


def along_z(block, shift):
    route = [
        (tile_of(z, y, core), tile_of(z + shift, y, core))
        for z, y, core in places()
        if 0 <= z + shift < 8
    ]
    return lax.ppermute(block, "tok", route)


def row_of_tiles(block):
    blocks = block[None]
    for bit in (1, 2, 4):
        route = [(i, i ^ bit) for i in range(TILES)]
        blocks = jnp.concatenate([blocks, lax.ppermute(blocks, "tok", route)])
    return blocks


def both_ways(move, behind, ahead):
    middle = behind.shape[-1] // 2
    return jnp.concatenate([move(behind[..., :middle], 1), move(ahead[..., middle:], 3)], axis=-1)


def pack_gains(gains):
    high = lax.reduce_precision(gains, 8, 7)
    rest = gains - high
    middle = lax.reduce_precision(rest, 8, 7)
    terms = jnp.concatenate([high, middle, rest - middle]).astype(BF16)
    return jnp.pad(terms, (0, 16 * 512 - terms.shape[0])).reshape(16, 512)


def unpack_gains(rows, count):
    terms = rows.reshape(-1, 16 * 512)[:, : 3 * count].reshape(-1, 3, count).astype(F32)
    return (terms[:, 0] + terms[:, 1]) + terms[:, 2]


def point_message(point_feats, point_voxel, send_counts):
    feats = point_feats.reshape(SECTIONS * TILES, SLOTS * CHANNELS)
    voxel = point_voxel.reshape(SECTIONS * TILES, SLOTS)
    counts = send_counts.reshape(SECTIONS * TILES, 1)
    live = jnp.arange(SLOTS)[None, :] < counts
    cell = jnp.where(live, voxel // 64 % SECTIONS * TOK_DEV + voxel // 256, -1).astype(BF16)
    inner = (voxel % 64).astype(BF16)
    return jnp.concatenate([feats, cell, inner, jnp.zeros((SECTIONS * TILES, 48), BF16)], axis=1)


def local(
    point_feats,
    point_voxel,
    send_counts,
    tok_weight,
    tok_gain,
    dec_weight,
    dec_gain,
    attn_gain,
    mlp_gain,
    query_gain,
    key_gain,
    qkv_weight,
    out_weight,
    in_weight,
    down_weight,
):
    place = jnp.stack([lax.axis_index("segment"), lax.axis_index("tok")]).astype(jnp.int32)
    tile = lax.axis_index("tok")
    core, y, z = tile % 2, tile // 2 % 4, tile // 8
    qkv, out, up, down = qkv_weight[0], out_weight[0], in_weight[0], down_weight[0]
    shifts = (1, 2, 3)

    c_piece = jnp.concatenate(
        [rows_of(weight, core * 256 + z * 32, 32) for weight in (up, out, dec_weight)], axis=1
    )
    e_piece = rows_of(down, core * 1024 + y * 256, 256)
    own_gains = jnp.concatenate([attn_gain, mlp_gain, query_gain, key_gain], axis=1)[0]
    t_piece = jnp.concatenate([rows_of(tok_weight, core * 256, 256), pack_gains(own_gains)])
    message = point_message(point_feats, point_voxel, send_counts)

    c_own = jnp.stack([along_x(c_piece, shift) for shift in shifts])
    t_near = [along_x(t_piece, 1), along_x(t_piece, 3)]
    c_own, e_piece, message, *t_near = together(c_own, e_piece, message, *t_near)

    c_mine = along_z_all(c_own)
    e_own = jnp.stack([along_x(e_piece, shift) for shift in shifts])
    t_mine = jnp.stack(t_near + [both_ways(along_x, *t_near)])
    points = lax.all_to_all(message, ("segment", "tok"), split_axis=0, concat_axis=0, tiled=True)
    a_piece = rows_of(qkv, core * 256, 256)
    e_own, t_mine, points, a_piece = together(e_own, t_mine, points, a_piece)

    t_other = sibling(t_mine)
    near = [along_y(e_own, 1), along_y(e_own, 3), along_x(a_piece, 1), along_x(a_piece, 3)]
    tiles = row_of_tiles(scatter(place, points, tok_gain[None], tok_weight, t_mine, t_other))
    near, tiles, e_own, a_piece = lax.optimization_barrier((near, tiles, e_own, a_piece))
    far = [along_y(e_own, 2), along_x(a_piece, 2)]
    blocks = [tiles if shift == 0 else along_z(tiles, shift) for shift in (2, 1, 0, -1, -2)]
    near, far, blocks, c_mine = lax.optimization_barrier((near, far, blocks, c_mine))

    gains = unpack_gains(t_mine[:, 256:], own_gains.shape[0])
    gains = jnp.concatenate([own_gains[None], gains[:1], gains[2:], gains[1:2]])
    query_gains = jnp.tile(gains[:, 1024:1088] * 0.125, (1, HEADS))
    key_gains = jnp.tile(gains[:, 1088:], (1, HEADS))
    weights = [qkv, out.reshape(16, 32, 512), up.reshape(16, 32, 2048), down]
    weights += [dec_weight.reshape(16, 32, 512), tok_weight, t_mine, t_other]
    for part in (near[2], near[3], far[1], c_mine, e_own, near[0], near[1], far[0]):
        weights += [part, sibling(part)]
    made = roll(
        place,
        jnp.concatenate([gains[:, :1024], query_gains, key_gains], axis=1),
        dec_gain[None],
        tok_gain[None],
        blocks,
        weights,
    )
    return place_scenes(place, [made[0]] + [along_x(made[shift], shift) for shift in (1, 2, 3)])


def solution(mesh):
    return jax.shard_map(
        local,
        mesh=mesh,
        in_specs=(
            P(None, ("segment", "tok"), None, None, None),
            P(None, ("segment", "tok"), None, None),
            P(None, ("segment", "tok"), None),
            P("segment", None),
            P(),
            P(None, "segment"),
            P(),
            P("segment", None),
            P("segment", None),
            P("segment", None),
            P("segment", None),
            P("segment", None, None),
            P("segment", None, None),
            P("segment", None, None),
            P("segment", None, None),
        ),
        out_specs=P(None, None, "tok", "segment"),
        check_vma=False,
    )
```
